32 devices in a mesh: groups: 2 (over y), blk: 16 (over z, x, core).
Axes of the slice: x: 2, y: 2, z: 4, core: 2. Of those that a mesh axis runs over, the one named last changes fastest.
Arguments:
- queries: bfloat16 [96, 8192], P(('groups', 'blk')), parts along dimension 0, may hold values from -6 to 6
- new_kv: bfloat16 [96, 2, 1024], P(('groups', 'blk')), parts along dimension 0, may hold values from -6 to 6
- cache_kv: bfloat16 [96, 2, 256, 1024], P(('groups', 'blk')), parts along dimension 0, may hold values from -6 to 6
- parents: int32 [96], P(('groups', 'blk')), parts along dimension 0, may hold values from 0 to 47, as said below
- residual: bfloat16 [8192, 96], P('blk', 'groups'), parts along dimension 1, may hold values from -6 to 6
- out_proj: bfloat16 [8192, 8192], P('blk'), may hold values from -0.0625 to 0.0625
- norm_gain: bfloat16 [8192], P('blk'), may hold values from 0.099609375 to 1.8984375
- w_gate: bfloat16 [20480, 8192], P('blk'), may hold values from -0.0625 to 0.0625
- w_up: bfloat16 [20480, 8192], P('blk'), may hold values from -0.0625 to 0.0625
- w_down: bfloat16 [8192, 20480], P(None, 'blk'), may hold values from -0.0625 to 0.0625
Outputs:
- after_attention: bfloat16 [8192, 96], P('blk', 'groups'), parts along dimension 1
- layer_out: bfloat16 [8192, 96], P('blk', 'groups'), parts along dimension 1
The draws below stay inside these ranges and needn't reach their ends.
There are 2 independent parts, one for each index of `groups`. The reference program is written for one: setup_inputs(seed, part) draws one part's arguments, and reference() takes and returns one part's arrays. A program takes and returns all parts, laid end to end along the dimension named above; an argument that names none is the same for every part. Nothing has to cross between parts.
Inputs may be any that keep to these rules, and one draw needn't show every extreme that they name: Rows and parents count from 0 within each part, and parents[r] lies among the 3 rows of r's own aligned block, from 3 * (r // 3) on.
All inputs are finite; a program needn't handle non-finite values.
Results may differ from the reference program's by a relative error of at most 0.012.
Values may be sent and summed in bfloat16 or wider, within the bound.
No kernel may reach another device: no remote copies, remote signals or barrier semaphores. Data moves between devices by JAX's collectives and lax.ppermute only.
A program may use at most 128 MiB of HBM per device.

```python
import math
import jax
import jax.numpy as jnp
from jax import lax

D = 8192
HQ = 64
KVH = 8
HD = 128
FF = 20480
CACHE = 256
R_DEV = 3
ROWS = 48


def common_parts(key):
    base_key = jax.random.fold_in(key, 11)
    query_base = jnp.clip(jax.random.normal(jax.random.fold_in(base_key, 1), (ROWS, HQ * HD), jnp.float32), -6.0, 6.0)
    return query_base


def draw_queries(key, part):
    query_base = common_parts(key)
    return query_base.astype(jnp.bfloat16)


def draw_new_kv(key, part):
    query_base = common_parts(key)
    query_sum = query_base.reshape(ROWS, KVH, HQ // KVH, HD).sum(axis=2).reshape(ROWS, KVH * HD)
    fresh_noise = jax.random.normal(jax.random.fold_in(key, 21), (ROWS, 2, KVH * HD), jnp.float32)
    new_key = jnp.clip(0.6 * fresh_noise[:, 0] + 0.35 * query_sum, -6.0, 6.0)
    new_value = jnp.clip(fresh_noise[:, 1], -6.0, 6.0)
    return jnp.stack([new_key, new_value], axis=1).astype(jnp.bfloat16)


def draw_cache_kv(key, part):
    fresh_noise = jnp.clip(jax.random.normal(jax.random.fold_in(key, 31), (ROWS, 2, CACHE, KVH * HD), jnp.float32), -6.0, 6.0)
    return fresh_noise.astype(jnp.bfloat16)


def draw_parents(key, part):
    offsets = jax.random.randint(jax.random.fold_in(key, 41), (ROWS,), 0, R_DEV)
    row_ids = jnp.arange(ROWS)
    offsets = jnp.where(row_ids == 0, 0, offsets)
    offsets = jnp.where(row_ids == ROWS - 1, R_DEV - 1, offsets)
    return (row_ids // R_DEV * R_DEV + offsets).astype(jnp.int32)


def strengthened(values, key, source, target, shards_of, factor):
    owner, partner = [(jnp.arange(values.shape[position]) // (values.shape[position] // shards_of)).reshape([-1 if axis == position else 1 for axis in range(values.ndim)]) for position in (source, target)]
    chosen = jax.random.permutation(key, shards_of)[partner]
    strong = (owner == chosen) | (owner == (partner + shards_of // 2) % shards_of)
    return jnp.where(strong, factor * values, values)


def steps_of(key, shape, pieces, least, largest):
    loudness = 1.0
    for dim, shards_of in pieces:
        heights = jax.random.uniform(jax.random.fold_in(jax.random.fold_in(key, 6), dim), (shards_of,), jnp.float32, least / len(pieces), largest / len(pieces))
        loudness = loudness * jnp.repeat(jnp.exp(heights), shape[dim] // shards_of).reshape((-1,) + (1,) * (len(shape) - 1 - dim))
    return loudness


def normal_values(own_key, extent, width, bound, pieces=(), held_as=jnp.bfloat16):
    level = steps_of(own_key, extent, pieces, -0.22, 0.18) if pieces else 1.0
    drawn = jax.random.normal(own_key, extent, jnp.float32) * width * level
    return jnp.minimum(jnp.maximum(drawn, -bound), bound).astype(held_as)


def heavy_noise(rng, shape, scale, reach, pieces, heavy, kind=jnp.bfloat16):
    entries = scale * jax.random.normal(rng, shape, jnp.float32)
    if pieces:
        entries = entries * steps_of(rng, shape, pieces, -0.22, 0.18)
    return jnp.clip(strengthened(entries, jax.random.fold_in(rng, 3), *heavy), -reach, reach).astype(kind)


def setup_inputs(seed: int = 0, part: int = 0) -> dict:
    key_list = jax.random.split(jax.random.key(seed), 11)
    part_splits = jax.random.split(jax.random.fold_in(key_list[10], part), 11)
    return {
        "queries": draw_queries(jax.random.fold_in(jax.random.fold_in(key_list[10], part), 71), part),
        "new_kv": draw_new_kv(jax.random.fold_in(jax.random.fold_in(key_list[10], part), 71), part),
        "cache_kv": draw_cache_kv(jax.random.fold_in(jax.random.fold_in(key_list[10], part), 71), part),
        "parents": draw_parents(jax.random.fold_in(jax.random.fold_in(key_list[10], part), 71), part),
        "residual": normal_values(part_splits[4], (D, ROWS), 1.0, 6.0, ((0, 16),)),
        "out_proj": normal_values(key_list[5], (D, HQ * HD), (HQ * HD) ** -0.5, 0.0625, ((0, 16),)),
        "norm_gain": jnp.clip(1.0 + 0.18 * jax.random.normal(key_list[6], (D,), jnp.float32), 0.099609375, 1.8984375).astype(jnp.bfloat16),
        "w_gate": normal_values(key_list[7], (FF, D), D ** -0.5, 0.0625, ((0, 16),)),
        "w_up": normal_values(key_list[8], (FF, D), D ** -0.5, 0.0625, ((0, 16),)),
        "w_down": heavy_noise(key_list[9], (D, FF), FF ** -0.5, 0.0625, ((1, 16),), (1, 0, 16, 2.0)),
    }


def one_row(cache_kv, operands):
    query_row, new_row, parent_row = operands
    group_size = HQ // KVH
    picked = cache_kv[parent_row]
    key_all = jnp.concatenate([picked[0], new_row[0][None, :]], axis=0).reshape(CACHE + 1, KVH, HD)
    value_all = jnp.concatenate([picked[1], new_row[1][None, :]], axis=0).reshape(CACHE + 1, KVH, HD)
    query_heads = query_row.reshape(KVH, group_size, HD)
    score_all = jnp.einsum('gjd,cgd->gjc', query_heads.astype(jnp.float32), key_all.astype(jnp.float32)) * (1.0 / math.sqrt(HD))
    score_top = lax.optimization_barrier(jnp.max(score_all, axis=-1, keepdims=True))
    expo = jnp.exp(score_all - score_top)
    weights = (expo / lax.optimization_barrier(jnp.sum(expo, axis=-1, keepdims=True))).astype(jnp.bfloat16)
    mixed_heads = jnp.einsum('gjc,cgd->gjd', weights.astype(jnp.float32), value_all.astype(jnp.float32))
    return mixed_heads.reshape(HQ * HD).astype(jnp.bfloat16)

def reference(queries, new_kv, cache_kv, parents, residual, out_proj, norm_gain, w_gate, w_up, w_down):
    attended = lax.map(lambda operands: one_row(cache_kv, operands), (queries, new_kv, parents.astype(jnp.int32)))
    projected = jnp.dot(out_proj, attended.T, preferred_element_type=jnp.float32)
    after_attention = (residual.astype(jnp.float32) + projected).astype(jnp.bfloat16)
    widened = after_attention.astype(jnp.float32)
    inverse_rms = lax.rsqrt(lax.optimization_barrier(jnp.sum(widened * widened, axis=0)) / D + 1e-06)
    normed = (widened * inverse_rms[None, :] * norm_gain.astype(jnp.float32)[:, None]).astype(jnp.bfloat16)
    gate_sum = jnp.dot(w_gate, normed, preferred_element_type=jnp.float32)
    up_sum = jnp.dot(w_up, normed, preferred_element_type=jnp.float32)
    hidden = (jax.nn.silu(gate_sum) * up_sum).astype(jnp.bfloat16)
    ffn_delta = jnp.dot(w_down, hidden, preferred_element_type=jnp.float32)
    layer_out = (widened + ffn_delta).astype(jnp.bfloat16)
    return (after_attention, layer_out)
```

```python
import functools
import math

import jax
import jax.numpy as jnp
from jax import lax
from jax.experimental import pallas as pl
from jax.experimental.pallas import tpu as pltpu
from jax.sharding import PartitionSpec as P

D = 8192
HQ = 64
KVH = 8
HD = 128
CACHE = 256
GAIN_ROWS = 16

epsilon = 1e-06
F32 = jnp.float32
BF16 = jnp.bfloat16
NT = (((1,), (1,)), ((), ()))
VMEM = pl.BlockSpec(memory_space=pltpu.VMEM)
ANY = pl.BlockSpec(memory_space=pl.ANY)
SMEM = pl.BlockSpec(memory_space=pltpu.SMEM)


def attend_rows(queries, new_kv, cache_kv, parents):
    row_count = queries.shape[0]
    group_size = HQ // KVH
    local_parent = parents - lax.axis_index("blk") * row_count
    chosen = jnp.take(cache_kv, local_parent, axis=0)
    cache_keys = chosen[:, 0].reshape(row_count, CACHE, KVH, HD)
    cache_values = chosen[:, 1].reshape(row_count, CACHE, KVH, HD)
    new_key = new_kv[:, 0].reshape(row_count, KVH, HD)
    new_value = new_kv[:, 1].reshape(row_count, KVH, HD)
    query_heads = queries.reshape(row_count, KVH, group_size, HD)
    score_scale = 1.0 / math.sqrt(HD)
    score_cache = (
        jnp.einsum("rgjd,rcgd->rgjc", query_heads, cache_keys, preferred_element_type=jnp.float32)
        * score_scale
    )
    score_new = (
        jnp.einsum("rgjd,rgd->rgj", query_heads, new_key, preferred_element_type=jnp.float32)
        * score_scale
    )
    score_top = jnp.maximum(jnp.max(score_cache, axis=-1), score_new)
    expo_cache = jnp.exp(score_cache - score_top[..., None])
    expo_new = jnp.exp(score_new - score_top)
    denom_sum = jnp.sum(expo_cache, axis=-1) + expo_new
    weight_cache = (expo_cache / denom_sum[..., None]).astype(jnp.bfloat16)
    weight_new = (expo_new / denom_sum).astype(jnp.bfloat16)
    mixed_heads = jnp.einsum(
        "rgjc,rcgd->rgjd", weight_cache, cache_values, preferred_element_type=jnp.float32
    )
    mixed_heads = (
        mixed_heads
        + weight_new.astype(jnp.float32)[..., None] * new_value.astype(jnp.float32)[:, :, None, :]
    )
    return mixed_heads.reshape(row_count, HQ * HD).astype(jnp.bfloat16)


def plain_shards(queries, new_kv, cache_kv, parents, residual, out_proj, norm_gain, w_gate, w_up, w_down):
    attended = attend_rows(queries, new_kv, cache_kv, parents)
    projected = lax.dot_general(
        out_proj,
        lax.all_gather(attended, "blk", axis=0, tiled=True),
        (((1,), (1,)), ((), ())),
        preferred_element_type=jnp.float32,
    )
    after_attention = (residual.astype(jnp.float32) + projected).astype(jnp.bfloat16)
    widened = after_attention.astype(jnp.float32)
    gathered, gain_all = (
        lax.all_gather(after_attention, "blk", axis=0, tiled=True),
        lax.all_gather(norm_gain, "blk", axis=0, tiled=True),
    )
    gathered_wide = gathered.astype(jnp.float32)
    inverse_rms = lax.rsqrt(jnp.sum(gathered_wide * gathered_wide, axis=0) / D + epsilon)
    normed_all = (
        gathered_wide * inverse_rms[None, :] * gain_all.astype(jnp.float32)[:, None]
    ).astype(jnp.bfloat16)
    gate_sum = jnp.dot(w_gate, normed_all, preferred_element_type=jnp.float32)
    up_sum = jnp.dot(w_up, normed_all, preferred_element_type=jnp.float32)
    hidden = (jax.nn.silu(gate_sum) * up_sum).astype(jnp.bfloat16)
    ffn_delta = lax.psum_scatter(
        jnp.dot(w_down, hidden, preferred_element_type=jnp.float32),
        "blk",
        scatter_dimension=0,
        tiled=True,
    )
    layer_out = (widened + ffn_delta).astype(jnp.bfloat16)
    return (after_attention, layer_out)


class Exchange:
    def __init__(self, size):
        self.size = size
        bits = size.bit_length() - 1
        down = [1 << b for b in range(bits - 1, 0, -1)]
        other = list(down)
        if len(other) > 1:
            other[-1], other[-2] = other[-2], other[-1]
        self.masks = (other, down)
        self.half = size // 2

    def offset(self, core, p):
        return sum(m for k, m in enumerate(self.masks[core]) if p >> k & 1)

    def device(self, me, flip, p):
        core = (me & 1) ^ flip
        return (me ^ flip) ^ jnp.where(core == 1, self.offset(1, p), self.offset(0, p))

    def swap(self, x, stage):
        pairs = [(i, i ^ self.masks[i & 1][stage]) for i in range(self.size)]
        return lax.ppermute(x, "blk", pairs)

    def swap_core(self, x):
        return lax.ppermute(x, "blk", [(i, i ^ 1) for i in range(self.size)])

    def gather(self, x):
        pieces = []
        have = x
        parts = [x]
        count = 1
        fresh = x
        for stage in range(len(self.masks[0])):
            fresh = self.swap(have, stage)
            parts.append(fresh)
            if stage + 1 < len(self.masks[0]):
                have = jnp.concatenate([have, fresh])
        first = 0
        for k, part in enumerate(parts):
            count = part.shape[0] // x.shape[0]
            if k == 0:
                continue
            if k == 1:
                part = jnp.concatenate([x, part])
                count = 2
                first = 0
            pieces.append((part, 0, first, count))
            pieces.append((self.swap_core(part), 1, first, count))
            first += count
        return pieces


def attend_kernel(parents, queries, new_kv, gain, cache, out, held, sems):
    rows = held.shape[0]
    base = lax.axis_index("blk") * rows
    copies = [
        pltpu.make_async_copy(cache.at[parents[r] - base], held.at[r], sems.at[r]) for r in range(rows)
    ]
    for copy in copies:
        copy.start()
    scale = 1.0 / math.sqrt(HD)
    group = HQ // KVH
    width = KVH * HD
    head = lax.broadcasted_iota(jnp.int32, (HQ, width), 0) // group
    column = lax.broadcasted_iota(jnp.int32, (HQ, width), 1) // HD
    own = head == column
    out[rows * HQ :, :] = gain[...]
    for r in range(rows):
        query = queries[:, r, :].astype(F32)
        spread = jnp.where(own, jnp.concatenate([query] * KVH, axis=1), 0.0)
        new_key = new_kv[r, 0:1, :].astype(F32)
        new_value = new_kv[r, 1:2, :].astype(F32)
        score_new = jnp.sum(spread * new_key, axis=1, keepdims=True) * scale
        copies[r].wait()
        keys = held[r, 0]
        values = held[r, 1]
        score = lax.dot_general(spread.astype(BF16), keys, NT, preferred_element_type=F32) * scale
        top = jnp.maximum(jnp.max(score, axis=1, keepdims=True), score_new)
        expo = jnp.exp(score - top)
        expo_new = jnp.exp(score_new - top)
        total = jnp.sum(expo, axis=1, keepdims=True) + expo_new
        weight = (expo / total).astype(BF16)
        weight_new = (expo_new / total).astype(BF16).astype(F32)
        mixed = jnp.dot(weight, values, preferred_element_type=F32) + weight_new * new_value
        out[r * HQ : (r + 1) * HQ, :] = jnp.concatenate(
            [mixed[g * group : (g + 1) * group, g * HD : (g + 1) * HD] for g in range(KVH)], axis=0
        ).astype(BF16)


def attend(parents, queries, new_kv, cache_kv, norm_gain):
    rows = queries.shape[0]
    gain = jnp.zeros((GAIN_ROWS, HD), BF16)
    gain = lax.dynamic_update_slice(gain, norm_gain.reshape(-1, HD), (0, 0))
    return pl.pallas_call(
        attend_kernel,
        in_specs=[SMEM, VMEM, VMEM, VMEM, ANY],
        out_specs=VMEM,
        out_shape=jax.ShapeDtypeStruct((rows * HQ + GAIN_ROWS, HD), BF16),
        scratch_shapes=[
            pltpu.VMEM((rows, 2, CACHE, KVH * HD), BF16),
            pltpu.SemaphoreType.DMA((rows,)),
        ],
        compiler_params=pltpu.CompilerParams(vmem_limit_bytes=16 * 2**20),
        cost_estimate=pl.CostEstimate(flops=10**8, bytes_accessed=3 * 2**20, transcendentals=0),
        name="attend",
    )(parents, queries.reshape(rows, HQ, HD).transpose(1, 0, 2), new_kv, gain, cache_kv)


def project_kernel(exchange, layout, steps, *refs):
    pieces = refs[: len(layout)]
    residual, weight, out, wide, packed, held, sems = refs[len(layout) :]
    per_device = wide.shape[0] // exchange.size
    block = per_device + GAIN_ROWS
    beam_rows = out.shape[0]
    step = weight.shape[1] // steps
    copies = [
        pltpu.make_async_copy(weight.at[:, s * step : (s + 1) * step], held.at[s], sems.at[s])
        for s in range(steps)
    ]
    for copy in copies:
        copy.start()
    me = lax.axis_index("blk")
    for piece, (flip, first, count) in zip(pieces, layout):
        for k in range(count):
            device = exchange.device(me, flip, first + k)
            start = pl.multiple_of(device * per_device, per_device)
            wide[pl.ds(start, per_device), :] = piece[k * block : k * block + per_device, :].astype(F32)
    for h in range(HQ):
        packed[:, h * HD : (h + 1) * HD] = wide[pl.ds(h, beam_rows, stride=HQ), :].astype(BF16)
    total = residual[...].astype(F32)
    summed = None
    for s in range(steps):
        copies[s].wait()
        term = lax.dot_general(
            packed[:, s * step : (s + 1) * step], held[s], NT, preferred_element_type=F32
        )
        summed = term if summed is None else summed + term
    out[...] = (total + summed).astype(BF16)


def project(exchange, pieces, residual, weight):
    beam_rows, features = residual.shape
    layout = [p[1:] for p in pieces]
    steps = 4
    per_device = beam_rows * HQ // exchange.size
    return pl.pallas_call(
        functools.partial(project_kernel, exchange, layout, steps),
        in_specs=[VMEM] * len(pieces) + [VMEM, ANY],
        out_specs=VMEM,
        out_shape=jax.ShapeDtypeStruct((beam_rows, features), BF16),
        scratch_shapes=[
            pltpu.VMEM((beam_rows * HQ, HD), F32),
            pltpu.VMEM((beam_rows, HQ * HD), BF16),
            pltpu.VMEM((steps, features, weight.shape[1] // steps), BF16),
            pltpu.SemaphoreType.DMA((steps,)),
        ],
        compiler_params=pltpu.CompilerParams(vmem_limit_bytes=24 * 2**20),
        cost_estimate=pl.CostEstimate(flops=4 * 10**8, bytes_accessed=9 * 2**20, transcendentals=0),
        name="project",
    )(*[p[0] for p in pieces], residual, weight)


def feed_kernel(exchange, layout, gate_slots, down_slots, *refs):
    blocks = refs[: len(layout)]
    gains = refs[len(layout) : 2 * len(layout)]
    (gate, up, down, keep, send, normed, gate_held, up_held, down_held, gate_sum, up_sum, hidden,
     gate_sems, up_sems, down_sems) = refs[2 * len(layout) :]
    size = exchange.size
    pairs = size // 2
    half_pairs = size // 4
    beam_rows, features = keep.shape[1:]
    gain_block = gains[0].shape[0] // layout[0][2]
    me = lax.axis_index("blk")
    owners = [(flip, first + k) for flip, first, count in layout for k in range(count)]

    def gate_copies(q):
        s = q % gate_slots
        made = []
        for j in range(2):
            device = exchange.device(me, *owners[2 * q + j])
            columns = pl.ds(pl.multiple_of(device * features, features), features)
            place = pl.ds(j * features, features)
            made.append(pltpu.make_async_copy(gate.at[:, columns], gate_held.at[s, :, place], gate_sems.at[s, j]))
            made.append(pltpu.make_async_copy(up.at[:, columns], up_held.at[s, :, place], up_sems.at[s, j]))
        return made

    def down_copies(q):
        s = q % down_slots
        flip, first = (1, 2 * q) if q < half_pairs else (0, 2 * (q - half_pairs))
        made = []
        for j in range(2):
            device = exchange.device(me, flip, first + j)
            rows = pl.ds(pl.multiple_of(device * features, features), features)
            place = pl.ds(j * features, features)
            made.append(pltpu.make_async_copy(down.at[rows, :], down_held.at[s, place, :], down_sems.at[s, j]))
        return made

    for q in range(gate_slots):
        for copy in gate_copies(q):
            copy.start()
    for q in range(down_slots):
        for copy in down_copies(q):
            copy.start()

    squares = jnp.zeros((beam_rows, 1), F32)
    n = 0
    for block, gain, (flip, first, count) in zip(blocks, gains, layout):
        for k in range(count):
            for j in range(features // HD):
                value = block[k * beam_rows : (k + 1) * beam_rows, j * HD : (j + 1) * HD].astype(F32)
                squares += jnp.sum(value * value, axis=1, keepdims=True)
                row = k * gain_block + gain_block - GAIN_ROWS + j
                scaled = value * gain[row : row + 1, :].astype(F32)
                place = (n % 2) * features + j * HD
                normed[n // 2, :, place : place + HD] = scaled.astype(BF16)
            n += 1
    inverse_rms = lax.rsqrt(squares / (size * features) + epsilon)

    for q in range(pairs):
        s = q % gate_slots
        for copy in gate_copies(q):
            copy.wait()
        term = lax.dot_general(normed[q], gate_held[s], NT, preferred_element_type=F32)
        gate_sum[...] = term if q == 0 else gate_sum[...] + term
        term = lax.dot_general(normed[q], up_held[s], NT, preferred_element_type=F32)
        up_sum[...] = term if q == 0 else up_sum[...] + term
        if q + gate_slots < pairs:
            for copy in gate_copies(q + gate_slots):
                copy.start()
    hidden[...] = (jax.nn.silu(gate_sum[...] * inverse_rms) * (up_sum[...] * inverse_rms)).astype(BF16)
    for q in range(pairs):
        s = q % down_slots
        for copy in down_copies(q):
            copy.wait()
        term = lax.dot_general(hidden[...], down_held[s], NT, preferred_element_type=F32)
        for j in range(2):
            part = term[:, j * features : (j + 1) * features]
            if q < half_pairs:
                send[2 * q + j] = part.astype(BF16)
            else:
                keep[2 * (q - half_pairs) + j] = part
        if q + down_slots < pairs:
            for copy in down_copies(q + down_slots):
                copy.start()


def feed(exchange, blocks, gains, gate, up, down):
    layout = [b[1:] for b in blocks]
    beam_rows = blocks[0][0].shape[0] // blocks[0][3]
    features = blocks[0][0].shape[1]
    units = gate.shape[0]
    gate_slots, down_slots = min(6, exchange.size // 2), min(4, exchange.size // 2)
    return pl.pallas_call(
        functools.partial(feed_kernel, exchange, layout, gate_slots, down_slots),
        in_specs=[VMEM] * (2 * len(blocks)) + [ANY] * 3,
        out_specs=[VMEM, VMEM],
        out_shape=[
            jax.ShapeDtypeStruct((exchange.half, beam_rows, features), F32),
            jax.ShapeDtypeStruct((exchange.half, beam_rows, features), BF16),
        ],
        scratch_shapes=[
            pltpu.VMEM((exchange.size // 2, beam_rows, 2 * features), BF16),
            pltpu.VMEM((gate_slots, units, 2 * features), BF16),
            pltpu.VMEM((gate_slots, units, 2 * features), BF16),
            pltpu.VMEM((down_slots, 2 * features, units), BF16),
            pltpu.VMEM((beam_rows, units), F32),
            pltpu.VMEM((beam_rows, units), F32),
            pltpu.VMEM((beam_rows, units), BF16),
            pltpu.SemaphoreType.DMA((gate_slots, 2)),
            pltpu.SemaphoreType.DMA((gate_slots, 2)),
            pltpu.SemaphoreType.DMA((down_slots, 2)),
        ],
        compiler_params=pltpu.CompilerParams(vmem_limit_bytes=56 * 2**20),
        cost_estimate=pl.CostEstimate(flops=3 * 10**9, bytes_accessed=62 * 2**20, transcendentals=0),
        name="feed",
    )(*[b[0] for b in blocks], *[g[0] for g in gains], gate, up, down)


def scatter_sum(exchange, keep, send):
    keep = keep + exchange.swap_core(send).astype(F32)
    for stage in range(len(exchange.masks[0]) - 1, -1, -1):
        half = keep.shape[0] // 2
        keep = keep[:half] + exchange.swap(keep[half:].astype(BF16), stage).astype(F32)
    return keep[0]


def fast_shards(size, queries, new_kv, cache_kv, parents, residual, out_proj, norm_gain, w_gate, w_up, w_down):
    exchange = Exchange(size)
    mixed = attend(parents, queries, new_kv, cache_kv, norm_gain)
    pieces = exchange.gather(mixed)
    after = project(exchange, pieces, residual.T, out_proj)
    blocks = exchange.gather(after)
    keep, send = feed(exchange, blocks, pieces, w_gate, w_up, w_down)
    delta = scatter_sum(exchange, keep, send)
    layer_out = (after.astype(F32) + delta).astype(BF16)
    return (after.T, layer_out.T)


def solution(mesh):
    size = mesh.shape["blk"]

    def shards(*args):
        features, beam_rows = args[4].shape
        units = args[7].shape[0]
        fits = (
            size >= 8
            and size & (size - 1) == 0
            and features % HD == 0
            and features // HD <= GAIN_ROWS
            and beam_rows % 16 == 0
            and beam_rows * HQ * HD <= 2**20
            and units % HD == 0
            and units * features <= 2**20
        )
        return functools.partial(fast_shards, size)(*args) if fits else plain_shards(*args)

    return jax.shard_map(
        shards,
        mesh=mesh,
        in_specs=(
            P(("groups", "blk"), None),
            P(("groups", "blk"), None, None),
            P(("groups", "blk"), None, None, None),
            P(("groups", "blk")),
            P("blk", "groups"),
            P("blk", None),
            P("blk"),
            P("blk", None),
            P("blk", None),
            P(None, "blk"),
        ),
        out_specs=(P("blk", "groups"), P("blk", "groups")),
        check_vma=False,
    )
```

```python
import functools
import math

import jax
import jax.numpy as jnp
from jax import lax
from jax.experimental import pallas as pl
from jax.experimental.pallas import tpu as pltpu
from jax.sharding import PartitionSpec as P

D = 8192
HQ = 64
KVH = 8
HD = 128
CACHE = 256
GAIN_ROWS = 16

epsilon = 1e-06
F32 = jnp.float32
BF16 = jnp.bfloat16
NT = (((1,), (1,)), ((), ()))
VMEM = pl.BlockSpec(memory_space=pltpu.VMEM)
ANY = pl.BlockSpec(memory_space=pl.ANY)
SMEM = pl.BlockSpec(memory_space=pltpu.SMEM)


def attend_rows(queries, new_kv, cache_kv, parents):
    row_count = queries.shape[0]
    group_size = HQ // KVH
    local_parent = parents - lax.axis_index("blk") * row_count
    chosen = jnp.take(cache_kv, local_parent, axis=0)
    cache_keys = chosen[:, 0].reshape(row_count, CACHE, KVH, HD)
    cache_values = chosen[:, 1].reshape(row_count, CACHE, KVH, HD)
    new_key = new_kv[:, 0].reshape(row_count, KVH, HD)
    new_value = new_kv[:, 1].reshape(row_count, KVH, HD)
    query_heads = queries.reshape(row_count, KVH, group_size, HD)
    score_scale = 1.0 / math.sqrt(HD)
    score_cache = (
        jnp.einsum("rgjd,rcgd->rgjc", query_heads, cache_keys, preferred_element_type=jnp.float32)
        * score_scale
    )
    score_new = (
        jnp.einsum("rgjd,rgd->rgj", query_heads, new_key, preferred_element_type=jnp.float32)
        * score_scale
    )
    score_top = jnp.maximum(jnp.max(score_cache, axis=-1), score_new)
    expo_cache = jnp.exp(score_cache - score_top[..., None])
    expo_new = jnp.exp(score_new - score_top)
    denom_sum = jnp.sum(expo_cache, axis=-1) + expo_new
    weight_cache = (expo_cache / denom_sum[..., None]).astype(jnp.bfloat16)
    weight_new = (expo_new / denom_sum).astype(jnp.bfloat16)
    mixed_heads = jnp.einsum(
        "rgjc,rcgd->rgjd", weight_cache, cache_values, preferred_element_type=jnp.float32
    )
    mixed_heads = (
        mixed_heads
        + weight_new.astype(jnp.float32)[..., None] * new_value.astype(jnp.float32)[:, :, None, :]
    )
    return mixed_heads.reshape(row_count, HQ * HD).astype(jnp.bfloat16)


def plain_shards(queries, new_kv, cache_kv, parents, residual, out_proj, norm_gain, w_gate, w_up, w_down):
    attended = attend_rows(queries, new_kv, cache_kv, parents)
    projected = lax.dot_general(
        out_proj,
        lax.all_gather(attended, "blk", axis=0, tiled=True),
        (((1,), (1,)), ((), ())),
        preferred_element_type=jnp.float32,
    )
    after_attention = (residual.astype(jnp.float32) + projected).astype(jnp.bfloat16)
    widened = after_attention.astype(jnp.float32)
    gathered, gain_all = (
        lax.all_gather(after_attention, "blk", axis=0, tiled=True),
        lax.all_gather(norm_gain, "blk", axis=0, tiled=True),
    )
    gathered_wide = gathered.astype(jnp.float32)
    inverse_rms = lax.rsqrt(jnp.sum(gathered_wide * gathered_wide, axis=0) / D + epsilon)
    normed_all = (
        gathered_wide * inverse_rms[None, :] * gain_all.astype(jnp.float32)[:, None]
    ).astype(jnp.bfloat16)
    gate_sum = jnp.dot(w_gate, normed_all, preferred_element_type=jnp.float32)
    up_sum = jnp.dot(w_up, normed_all, preferred_element_type=jnp.float32)
    hidden = (jax.nn.silu(gate_sum) * up_sum).astype(jnp.bfloat16)
    ffn_delta = lax.psum_scatter(
        jnp.dot(w_down, hidden, preferred_element_type=jnp.float32),
        "blk",
        scatter_dimension=0,
        tiled=True,
    )
    layer_out = (widened + ffn_delta).astype(jnp.bfloat16)
    return (after_attention, layer_out)


class Exchange:
    def __init__(self, size):
        self.size = size
        bits = size.bit_length() - 1
        down = [1 << b for b in range(bits - 1, 0, -1)]
        other = list(down)
        if len(other) > 1:
            other[-1], other[-2] = other[-2], other[-1]
        self.masks = (other, down)
        self.half = size // 2

    def offset(self, core, p):
        return sum(m for k, m in enumerate(self.masks[core]) if p >> k & 1)

    def device(self, me, flip, p):
        core = (me & 1) ^ flip
        return (me ^ flip) ^ jnp.where(core == 1, self.offset(1, p), self.offset(0, p))

    def swap(self, x, stage):
        pairs = [(i, i ^ self.masks[i & 1][stage]) for i in range(self.size)]
        return lax.ppermute(x, "blk", pairs)

    def swap_core(self, x):
        return lax.ppermute(x, "blk", [(i, i ^ 1) for i in range(self.size)])


def attend_kernel(
    exchange, parents, queries, new_kv, gain, cache, gate, up, out, gate_out, up_out,
    chosen, asked, fresh, scaling, held, small_sems, sems, ahead_sems,
):
    rows = held.shape[0]
    base = lax.axis_index("blk") * rows
    first = pltpu.make_async_copy(parents, chosen, small_sems.at[0])
    others = [
        pltpu.make_async_copy(source, target, small_sems.at[k + 1])
        for k, (source, target) in enumerate([(queries, asked), (new_kv, fresh), (gain, scaling)])
    ]
    first.start()
    for copy in others:
        copy.start()
    first.wait()
    copies = [
        pltpu.make_async_copy(cache.at[chosen[r] - base], held.at[r], sems.at[r]) for r in range(rows)
    ]
    for copy in copies:
        copy.start()
    ahead = column_copies(exchange, [(0, 0)], gate, up, gate_out, up_out, ahead_sems)
    for copy in ahead:
        copy.start()
    scale = 1.0 / math.sqrt(HD)
    group = HQ // KVH
    width = KVH * HD
    head = lax.broadcasted_iota(jnp.int32, (HQ, width), 0) // group
    column = lax.broadcasted_iota(jnp.int32, (HQ, width), 1) // HD
    own = head == column
    for copy in others:
        copy.wait()
    gain_rows = scaling.shape[0]
    out[rows * HQ :, :] = jnp.concatenate(
        [scaling[...].astype(F32), jnp.zeros((GAIN_ROWS - gain_rows, HD), F32)], axis=0
    ).astype(BF16)
    for r in range(rows):
        query = asked[:, r, :].astype(F32)
        spread = jnp.where(own, jnp.concatenate([query] * KVH, axis=1), 0.0)
        new_key = fresh[r, 0:1, :].astype(F32)
        new_value = fresh[r, 1:2, :].astype(F32)
        score_new = jnp.sum(spread * new_key, axis=1, keepdims=True) * scale
        copies[r].wait()
        keys = held[r, 0]
        values = held[r, 1]
        score = lax.dot_general(spread.astype(BF16), keys, NT, preferred_element_type=F32) * scale
        top = jnp.maximum(jnp.max(score, axis=1, keepdims=True), score_new)
        expo = jnp.exp(score - top)
        expo_new = jnp.exp(score_new - top)
        total = jnp.sum(expo, axis=1, keepdims=True) + expo_new
        weight = (expo / total).astype(BF16)
        weight_new = (expo_new / total).astype(BF16).astype(F32)
        mixed = jnp.dot(weight, values, preferred_element_type=F32) + weight_new * new_value
        out[r * HQ : (r + 1) * HQ, :] = jnp.concatenate(
            [mixed[g * group : (g + 1) * group, g * HD : (g + 1) * HD] for g in range(KVH)], axis=0
        ).astype(BF16)
    for copy in ahead:
        copy.wait()


def in_hbm(x):
    return pltpu.with_memory_space_constraint(x, pltpu.HBM)


def attend(exchange, parents, queries, new_kv, cache_kv, norm_gain, gate, up):
    rows = queries.shape[0]
    features = norm_gain.shape[0]
    gain = norm_gain.reshape(-1, HD)
    queries = queries.reshape(rows, HQ, HD).transpose(1, 0, 2)
    ahead = held_shape(gate, features, 1)
    return pl.pallas_call(
        functools.partial(attend_kernel, exchange),
        in_specs=[ANY] * 7,
        out_specs=[VMEM] * 3,
        out_shape=[pltpu.VMEM((rows * HQ + GAIN_ROWS, HD), BF16), ahead, ahead],
        scratch_shapes=[
            pltpu.SMEM(parents.shape, parents.dtype),
            pltpu.VMEM(queries.shape, BF16),
            pltpu.VMEM(new_kv.shape, BF16),
            pltpu.VMEM(gain.shape, BF16),
            pltpu.VMEM((rows, 2, CACHE, KVH * HD), BF16),
            pltpu.SemaphoreType.DMA((4,)),
            pltpu.SemaphoreType.DMA((rows,)),
            pltpu.SemaphoreType.DMA((2,)),
        ],
        compiler_params=pltpu.CompilerParams(vmem_limit_bytes=16 * 2**20),
        cost_estimate=pl.CostEstimate(flops=10**8, bytes_accessed=3 * 2**20, transcendentals=0),
        name="attend",
    )(*[in_hbm(x) for x in (parents, queries, new_kv, gain, cache_kv, gate, up)])


def held_shape(gate, features, count):
    return pltpu.VMEM(((count + 1) // 2, gate.shape[0], features * min(count, 2)), BF16)


def column_copies(exchange, owners, gate, up, gate_held, up_held, sems):
    me = lax.axis_index("blk")
    features = gate.shape[1] // exchange.size
    copies = []
    for n, (flip, p) in enumerate(owners):
        device = exchange.device(me, flip, p)
        columns = pl.ds(pl.multiple_of(device * features, features), features)
        place = pl.ds(n % 2 * features, features)
        for k, (source, target) in enumerate(((gate, gate_held), (up, up_held))):
            copies.append(
                pltpu.make_async_copy(source.at[:, columns], target.at[n // 2, :, place], sems.at[2 * n + k])
            )
    return copies


def join_kernel(count, *refs):
    out = refs[-1]
    first = 0
    for part in refs[:count]:
        out[first : first + part.shape[0], :] = part[...]
        first += part.shape[0]


def join(parts, *after):
    rows = sum(p.shape[0] for p in parts)
    return pl.pallas_call(
        functools.partial(join_kernel, len(parts)),
        in_specs=[VMEM] * len(parts) + [ANY] * len(after),
        out_specs=VMEM,
        out_shape=pltpu.VMEM((rows,) + parts[0].shape[1:], parts[0].dtype),
        compiler_params=pltpu.CompilerParams(vmem_limit_bytes=2**20),
        name="join",
    )(*parts, *after)


def load_kernel(exchange, layout, unused, source, out, sems):
    if layout is None:
        copies = [pltpu.make_async_copy(source, out, sems.at[0])]
    else:
        copies = row_copies(exchange, layout, source, out, sems)
    for copy in copies:
        copy.start()
    for copy in copies:
        copy.wait()


def row_copies(exchange, layout, source, out, sems):
    me = lax.axis_index("blk")
    flip, first, count = layout
    rows = source.shape[0] // exchange.size
    copies = []
    for k in range(count):
        device = exchange.device(me, flip, first + k)
        start = pl.multiple_of(device * rows, rows)
        place = pl.ds(k * rows, rows)
        copies.append(pltpu.make_async_copy(source.at[pl.ds(start, rows), :], out.at[place, :], sems.at[k]))
    return copies


def load(exchange, layout, after, source):
    rows = source.shape[0] if layout is None else source.shape[0] // exchange.size * layout[2]
    shape = (rows, source.shape[1])
    return pl.pallas_call(
        functools.partial(load_kernel, exchange, layout),
        in_specs=[ANY, ANY],
        out_specs=VMEM,
        out_shape=pltpu.VMEM(shape, source.dtype),
        scratch_shapes=[pltpu.SemaphoreType.DMA((1 if layout is None else layout[2],))],
        compiler_params=pltpu.CompilerParams(vmem_limit_bytes=2**20),
        cost_estimate=pl.CostEstimate(flops=0, bytes_accessed=2 * rows * source.shape[1], transcendentals=0),
        name="load",
    )(after, in_hbm(source))


def project_kernel(exchange, layout, fetch, steps, *refs):
    pieces = refs[: len(layout)]
    residual, weight, down, out, copy_out, gains = refs[len(layout) : len(layout) + 6]
    fetched = refs[len(layout) + 6 : len(layout) + 6 + len(fetch)]
    wide, packed, stream, stream_sem, *fetch_sems = refs[len(layout) + 6 + len(fetch) :]
    per_device = wide.shape[0] // exchange.size
    block = per_device + GAIN_ROWS
    beam_rows = out.shape[0]
    step = weight.shape[1] // steps
    stream_copy = pltpu.make_async_copy(residual, stream, stream_sem)
    stream_copy.start()
    fetches = [
        copy
        for rows, target, sems in zip(fetch, fetched, fetch_sems)
        for copy in row_copies(exchange, rows, down, target, sems)
    ]
    for copy in fetches:
        copy.start()
    me = lax.axis_index("blk")
    for piece, (flip, first, count) in zip(pieces, layout):
        for k in range(count):
            device = exchange.device(me, flip, first + k)
            start = pl.multiple_of(device * per_device, per_device)
            wide[pl.ds(start, per_device), :] = piece[k * block : k * block + per_device, :].astype(F32)
            rows = piece[k * block + per_device : (k + 1) * block, :].astype(F32)
            slot = flip * exchange.half + first + k
            gains[slot : slot + 1, :] = jnp.concatenate(
                [rows[j : j + 1, :] for j in range(gains.shape[1] // HD)], axis=1
            )
    for h in range(HQ):
        packed[:, h * HD : (h + 1) * HD] = wide[pl.ds(h, beam_rows, stride=HQ), :].astype(BF16)
    summed = None
    for s in range(steps):
        part = slice(s * step, (s + 1) * step)
        term = lax.dot_general(packed[:, part], weight[:, part], NT, preferred_element_type=F32)
        summed = term if summed is None else summed + term
    stream_copy.wait()
    result = (stream[...].astype(F32) + summed).astype(BF16)
    out[...] = result
    copy_out[...] = result
    for copy in fetches:
        copy.wait()


def project(exchange, pieces, residual, weight, down, fetch):
    beam_rows, features = residual.shape
    layout = [p[1:] for p in pieces]
    rows = down.shape[0] // exchange.size
    return pl.pallas_call(
        functools.partial(project_kernel, exchange, layout, fetch, 4),
        in_specs=[VMEM] * len(pieces) + [ANY, VMEM, ANY],
        out_specs=[VMEM] * (3 + len(fetch)),
        out_shape=[
            jax.ShapeDtypeStruct((beam_rows, features), BF16),
            pltpu.VMEM((beam_rows, features), BF16),
            pltpu.VMEM((exchange.size, features), F32),
        ]
        + [pltpu.VMEM((rows * count, down.shape[1]), BF16) for _, _, count in fetch],
        scratch_shapes=[
            pltpu.VMEM((beam_rows * HQ, HD), F32),
            pltpu.VMEM((beam_rows, HQ * HD), BF16),
            pltpu.VMEM((beam_rows, features), BF16),
            pltpu.SemaphoreType.DMA,
        ]
        + [pltpu.SemaphoreType.DMA((count,)) for _, _, count in fetch],
        compiler_params=pltpu.CompilerParams(vmem_limit_bytes=8 * 2**20),
        cost_estimate=pl.CostEstimate(flops=4 * 10**8, bytes_accessed=9 * 2**20, transcendentals=0),
        name="project",
    )(*[p[0] for p in pieces], in_hbm(residual), weight, in_hbm(down))


def enter_kernel(exchange, layout, begun, early, ahead, *refs):
    refs = list(refs)
    take = lambda n: [refs.pop(0) for _ in range(n)]
    blocks = take(len(layout))
    (gains,) = take(1)
    sums = take(3) if begun else None
    early_held = take(2) if early else None
    gate, up = take(2)
    gate_sum, up_sum, squares = take(3)
    ahead_held = take(2) if ahead else None
    beam_rows, features = blocks[0].shape[0] // layout[0][2], blocks[0].shape[1]
    owners = [
        (block, k, flip, first + k) for block, (flip, first, count) in zip(blocks, layout) for k in range(count)
    ]
    copies = []
    late_held = None
    if early < len(owners):
        late_held = take(2)
        late = [(flip, p) for _, _, flip, p in owners[early:]]
        copies = column_copies(exchange, late, gate, up, *late_held, refs.pop(0))
    ahead_copies = column_copies(exchange, ahead, gate, up, *ahead_held, refs.pop(0)) if ahead else []
    for copy in copies + ahead_copies:
        copy.start()

    total = sums[2][...] if begun else jnp.zeros((beam_rows, features), F32)
    for n in range(0, len(owners), 2):
        pair = owners[n : n + 2]
        parts = []
        for block, k, flip, p in pair:
            value = block[k * beam_rows : (k + 1) * beam_rows, :].astype(F32)
            total += value * value
            slot = flip * exchange.half + p
            parts.append((value * gains[slot : slot + 1, :]).astype(BF16))
        normed = jnp.concatenate(parts, axis=1) if len(parts) > 1 else parts[0]
        depth = len(parts) * features
        for which, result in ((0, gate_sum), (1, up_sum)):
            if n < early:
                held = early_held[which][n // 2, :, :depth]
            else:
                for m in range(n - early, n - early + len(pair)):
                    copies[2 * m + which].wait()
                held = late_held[which][(n - early) // 2, :, :depth]
            term = lax.dot_general(normed, held, NT, preferred_element_type=F32)
            if n:
                result[...] += term
            elif begun:
                result[...] = sums[which][...] + term
            else:
                result[...] = term
    squares[...] = total
    for copy in ahead_copies:
        copy.wait()


def enter(exchange, blocks, gains, sums, early_held, gate, up, ahead=()):
    layout = [b[1:] for b in blocks]
    beam_rows, features = blocks[0][0].shape[0] // blocks[0][3], blocks[0][0].shape[1]
    units = gate.shape[0]
    count = sum(b[3] for b in blocks)
    early = 0
    if early_held:
        early = min(count, early_held[0].shape[0] * early_held[0].shape[2] // features)
    late = count - early
    out_shape = [
        pltpu.VMEM((beam_rows, units), F32),
        pltpu.VMEM((beam_rows, units), F32),
        pltpu.VMEM((beam_rows, features), F32),
    ]
    scratch = []
    if late:
        scratch += [held_shape(gate, features, late)] * 2 + [pltpu.SemaphoreType.DMA((2 * late,))]
    if ahead:
        out_shape += [held_shape(gate, features, len(ahead))] * 2
        scratch.append(pltpu.SemaphoreType.DMA((2 * len(ahead),)))
    operands = [b[0] for b in blocks] + [gains] + list(sums or ()) + list(early_held or ())
    in_specs = [VMEM] * len(operands) + [ANY] * 2
    return pl.pallas_call(
        functools.partial(enter_kernel, exchange, layout, sums is not None, early, ahead),
        in_specs=in_specs,
        out_specs=[VMEM] * len(out_shape),
        out_shape=out_shape,
        scratch_shapes=scratch,
        compiler_params=pltpu.CompilerParams(
            vmem_limit_bytes=(late + late % 2) * 4 * units * features + 4 * 2**20
        ),
        cost_estimate=pl.CostEstimate(
            flops=count * 4 * beam_rows * units * features,
            bytes_accessed=count * 4 * units * features,
            transcendentals=0,
        ),
        name="enter",
    )(*operands, in_hbm(gate), in_hbm(up))


def leave_kernel(first, *refs):
    if first:
        gate_sum, up_sum, squares, down, out, hidden = refs
        mean = jnp.sum(squares[...], axis=1, keepdims=True) / D
        inverse_rms = lax.rsqrt(mean + epsilon)
        hidden[...] = (jax.nn.silu(gate_sum[...] * inverse_rms) * (up_sum[...] * inverse_rms)).astype(BF16)
    else:
        hidden, down, *_, out = refs
    count, _, features = out.shape
    wide = 2 if count % 2 == 0 else 1
    for n in range(0, count, wide):
        term = lax.dot_general(
            hidden[...], down[n * features : (n + wide) * features, :], NT, preferred_element_type=F32
        )
        for j in range(wide):
            out[n + j] = term[:, j * features : (j + 1) * features].astype(out.dtype)


def leave(inputs, down, features, dtype, *after):
    first = len(inputs) == 3
    beam_rows, units = inputs[0].shape
    count = down.shape[0] // features
    out_shape = [pltpu.VMEM((count, beam_rows, features), dtype)]
    if first:
        out_shape.append(pltpu.VMEM((beam_rows, units), BF16))
    results = pl.pallas_call(
        functools.partial(leave_kernel, first),
        in_specs=[VMEM] * (len(inputs) + 1) + [ANY] * len(after),
        out_specs=[VMEM] * len(out_shape),
        out_shape=out_shape,
        compiler_params=pltpu.CompilerParams(vmem_limit_bytes=4 * 2**20),
        cost_estimate=pl.CostEstimate(
            flops=2 * count * beam_rows * units * features,
            bytes_accessed=2 * count * units * features,
            transcendentals=0,
        ),
        name="leave",
    )(*inputs, down, *after)
    return results if first else results[0]


def fast_shards(size, queries, new_kv, cache_kv, parents, residual, out_proj, norm_gain, w_gate, w_up, w_down):
    exchange = Exchange(size)
    features = residual.shape[0]
    high, low = (4, 4), (0, 4)

    mixed, *held = attend(exchange, parents, queries, new_kv, cache_kv, norm_gain, w_gate, w_up)
    fresh = exchange.swap(mixed, 0)
    high_send = load(exchange, (1,) + high, mixed, w_down)
    have = join([mixed, fresh], high_send)
    fresh = exchange.swap(have, 1)
    high_keep = load(exchange, (0,) + high, have, w_down)
    have = join([have, fresh], high_keep)
    fresh = exchange.swap(have, 2)
    weight = load(exchange, None, have, out_proj)
    have = join([have, fresh], weight)
    pieces = [(have, 0, 0, 8), (exchange.swap_core(have), 1, 0, 8)]
    after, have, gains, low_send, low_keep = project(
        exchange, pieces, residual.T, weight, w_down, [(1,) + low, (0,) + low]
    )

    block0 = have
    other0 = exchange.swap_core(block0)
    fresh1 = exchange.swap(block0, 0)
    *sums, g, u = enter(exchange, [(block0, 0, 0, 1)], gains, None, held, w_gate, w_up, [(0, 1), (1, 0)])
    have = join([block0, fresh1], sums[2])
    other1 = exchange.swap_core(fresh1)
    fresh2 = exchange.swap(have, 1)
    *sums, g, u = enter(
        exchange, [(fresh1, 0, 1, 1), (other0, 1, 0, 1)], gains, sums, [g, u], w_gate, w_up, [(0, 2), (0, 3)]
    )
    have = join([have, fresh2], sums[2])
    other2 = exchange.swap_core(fresh2)
    fresh3 = exchange.swap(have, 2)
    *sums, g, u = enter(
        exchange,
        [(fresh2, 0, 2, 2), (other1, 1, 1, 1)],
        gains, sums, [g, u], w_gate, w_up, [(1, 2), (1, 3), (0, 4), (0, 5)],
    )
    fresh3 = join([fresh3], sums[2])
    other3 = exchange.swap_core(fresh3)
    sums = enter(
        exchange, [(other2, 1, 2, 2), (fresh3, 0, 4, 4), (other3, 1, 4, 4)], gains, sums, [g, u], w_gate, w_up
    )

    send, hidden = leave(sums, high_send, features, BF16)
    received = exchange.swap_core(send).astype(F32)
    keep = leave((hidden,), high_keep, features, F32, send)
    onward = (keep + received).astype(BF16)
    passed = exchange.swap(onward, 2)
    send = leave((hidden,), low_send, features, BF16, onward)
    received = exchange.swap_core(send).astype(F32)
    keep = leave((hidden,), low_keep, features, F32, send)
    keep = keep + received + passed.astype(F32)
    for stage in (1, 0):
        part = keep.shape[0] // 2
        keep = keep[:part] + exchange.swap(keep[part:].astype(BF16), stage).astype(F32)
    layer_out = (after.astype(F32) + keep[0]).astype(BF16)
    return (after.T, layer_out.T)


def solution(mesh):
    size = mesh.shape["blk"]

    def shards(*args):
        features, beam_rows = args[4].shape
        units = args[7].shape[0]
        fits = (
            size == 16
            and features % HD == 0
            and features // HD <= GAIN_ROWS
            and beam_rows % 16 == 0
            and beam_rows * HQ * HD <= 2**20
            and units % HD == 0
            and units * features <= 2**20
        )
        return functools.partial(fast_shards, size)(*args) if fits else plain_shards(*args)

    return jax.shard_map(
        shards,
        mesh=mesh,
        in_specs=(
            P(("groups", "blk"), None),
            P(("groups", "blk"), None, None),
            P(("groups", "blk"), None, None, None),
            P(("groups", "blk")),
            P("blk", "groups"),
            P("blk", None),
            P("blk"),
            P("blk", None),
            P("blk", None),
            P(None, "blk"),
        ),
        out_specs=(P("blk", "groups"), P("blk", "groups")),
        check_vma=False,
    )
```

```python
import functools
import math

import jax
import jax.numpy as jnp
from jax import lax
from jax.experimental import pallas as pl
from jax.experimental.pallas import tpu as pltpu
from jax.sharding import PartitionSpec as P

D = 8192
HQ = 64
KVH = 8
HD = 128
CACHE = 256
GAIN_ROWS = 16

epsilon = 1e-06
F32 = jnp.float32
BF16 = jnp.bfloat16
NT = (((1,), (1,)), ((), ()))
VMEM = pl.BlockSpec(memory_space=pltpu.VMEM)
ANY = pl.BlockSpec(memory_space=pl.ANY)
SMEM = pl.BlockSpec(memory_space=pltpu.SMEM)


def attend_rows(queries, new_kv, cache_kv, parents):
    row_count = queries.shape[0]
    group_size = HQ // KVH
    local_parent = parents - lax.axis_index("blk") * row_count
    chosen = jnp.take(cache_kv, local_parent, axis=0)
    cache_keys = chosen[:, 0].reshape(row_count, CACHE, KVH, HD)
    cache_values = chosen[:, 1].reshape(row_count, CACHE, KVH, HD)
    new_key = new_kv[:, 0].reshape(row_count, KVH, HD)
    new_value = new_kv[:, 1].reshape(row_count, KVH, HD)
    query_heads = queries.reshape(row_count, KVH, group_size, HD)
    score_scale = 1.0 / math.sqrt(HD)
    score_cache = (
        jnp.einsum("rgjd,rcgd->rgjc", query_heads, cache_keys, preferred_element_type=jnp.float32)
        * score_scale
    )
    score_new = (
        jnp.einsum("rgjd,rgd->rgj", query_heads, new_key, preferred_element_type=jnp.float32)
        * score_scale
    )
    score_top = jnp.maximum(jnp.max(score_cache, axis=-1), score_new)
    expo_cache = jnp.exp(score_cache - score_top[..., None])
    expo_new = jnp.exp(score_new - score_top)
    denom_sum = jnp.sum(expo_cache, axis=-1) + expo_new
    weight_cache = (expo_cache / denom_sum[..., None]).astype(jnp.bfloat16)
    weight_new = (expo_new / denom_sum).astype(jnp.bfloat16)
    mixed_heads = jnp.einsum(
        "rgjc,rcgd->rgjd", weight_cache, cache_values, preferred_element_type=jnp.float32
    )
    mixed_heads = (
        mixed_heads
        + weight_new.astype(jnp.float32)[..., None] * new_value.astype(jnp.float32)[:, :, None, :]
    )
    return mixed_heads.reshape(row_count, HQ * HD).astype(jnp.bfloat16)


def plain_shards(queries, new_kv, cache_kv, parents, residual, out_proj, norm_gain, w_gate, w_up, w_down):
    attended = attend_rows(queries, new_kv, cache_kv, parents)
    projected = lax.dot_general(
        out_proj,
        lax.all_gather(attended, "blk", axis=0, tiled=True),
        (((1,), (1,)), ((), ())),
        preferred_element_type=jnp.float32,
    )
    after_attention = (residual.astype(jnp.float32) + projected).astype(jnp.bfloat16)
    widened = after_attention.astype(jnp.float32)
    gathered, gain_all = (
        lax.all_gather(after_attention, "blk", axis=0, tiled=True),
        lax.all_gather(norm_gain, "blk", axis=0, tiled=True),
    )
    gathered_wide = gathered.astype(jnp.float32)
    inverse_rms = lax.rsqrt(jnp.sum(gathered_wide * gathered_wide, axis=0) / D + epsilon)
    normed_all = (
        gathered_wide * inverse_rms[None, :] * gain_all.astype(jnp.float32)[:, None]
    ).astype(jnp.bfloat16)
    gate_sum = jnp.dot(w_gate, normed_all, preferred_element_type=jnp.float32)
    up_sum = jnp.dot(w_up, normed_all, preferred_element_type=jnp.float32)
    hidden = (jax.nn.silu(gate_sum) * up_sum).astype(jnp.bfloat16)
    ffn_delta = lax.psum_scatter(
        jnp.dot(w_down, hidden, preferred_element_type=jnp.float32),
        "blk",
        scatter_dimension=0,
        tiled=True,
    )
    layer_out = (widened + ffn_delta).astype(jnp.bfloat16)
    return (after_attention, layer_out)


class Exchange:
    def __init__(self, size):
        self.size = size
        bits = size.bit_length() - 1
        down = [1 << b for b in range(bits - 1, 0, -1)]
        other = list(down)
        if len(other) > 1:
            other[-1], other[-2] = other[-2], other[-1]
        self.masks = (other, down)
        self.half = size // 2

    def offset(self, core, p):
        return sum(m for k, m in enumerate(self.masks[core]) if p >> k & 1)

    def device(self, me, flip, p):
        core = (me & 1) ^ flip
        return (me ^ flip) ^ jnp.where(core == 1, self.offset(1, p), self.offset(0, p))

    def swap(self, x, stage):
        pairs = [(i, i ^ self.masks[i & 1][stage]) for i in range(self.size)]
        return lax.ppermute(x, "blk", pairs)

    def swap_core(self, x):
        return lax.ppermute(x, "blk", [(i, i ^ 1) for i in range(self.size)])


def apart(body):
    pl.when(lax.axis_index("blk") >= 0)(body)


def attend_kernel(parents, queries, new_kv, gain, cache, out, chosen, asked, fresh, scaling, held, small_sems, sems):
    rows = held.shape[0]
    base = lax.axis_index("blk") * rows
    others = [
        pltpu.make_async_copy(source, target, small_sems.at[k])
        for k, (source, target) in enumerate([(parents, chosen), (queries, asked), (new_kv, fresh), (gain, scaling)])
    ]
    copies = [pltpu.make_async_copy(cache.at[r], held.at[r], sems.at[r]) for r in range(rows)]
    for copy in others + copies:
        copy.start()
    scale = 1.0 / math.sqrt(HD)
    group = HQ // KVH
    width = KVH * HD

    @apart
    def _():
        head = lax.broadcasted_iota(jnp.int32, (HQ, width), 0) // group
        column = lax.broadcasted_iota(jnp.int32, (HQ, width), 1) // HD
        own = head == column
        for copy in others:
            copy.wait()
        gain_rows = scaling.shape[0]
        out[rows * HQ :, :] = jnp.concatenate(
            [scaling[...].astype(F32), jnp.zeros((GAIN_ROWS - gain_rows, HD), F32)], axis=0
        ).astype(BF16)
        for copy in copies:
            copy.wait()
        for r in range(rows):
            parent = chosen[r] - base
            query = asked[:, r, :].astype(F32)
            spread = jnp.where(own, jnp.concatenate([query] * KVH, axis=1), 0.0)
            new_key = fresh[r, 0:1, :].astype(F32)
            new_value = fresh[r, 1:2, :].astype(F32)
            score_new = jnp.sum(spread * new_key, axis=1, keepdims=True) * scale
            keys = held[parent, 0]
            values = held[parent, 1]
            score = lax.dot_general(spread.astype(BF16), keys, NT, preferred_element_type=F32) * scale
            top = jnp.maximum(jnp.max(score, axis=1, keepdims=True), score_new)
            expo = jnp.exp(score - top)
            expo_new = jnp.exp(score_new - top)
            total = jnp.sum(expo, axis=1, keepdims=True) + expo_new
            weight = (expo / total).astype(BF16)
            weight_new = (expo_new / total).astype(BF16).astype(F32)
            mixed = jnp.dot(weight, values, preferred_element_type=F32) + weight_new * new_value
            out[r * HQ : (r + 1) * HQ, :] = jnp.concatenate(
                [mixed[g * group : (g + 1) * group, g * HD : (g + 1) * HD] for g in range(KVH)], axis=0
            ).astype(BF16)


def in_hbm(x):
    return pltpu.with_memory_space_constraint(x, pltpu.HBM)


def attend(parents, queries, new_kv, cache_kv, norm_gain):
    rows = queries.shape[0]
    gain = norm_gain.reshape(-1, HD)
    queries = queries.reshape(rows, HQ, HD).transpose(1, 0, 2)
    return pl.pallas_call(
        attend_kernel,
        in_specs=[ANY] * 5,
        out_specs=VMEM,
        out_shape=pltpu.VMEM((rows * HQ + GAIN_ROWS, HD), BF16),
        scratch_shapes=[
            pltpu.SMEM(parents.shape, parents.dtype),
            pltpu.VMEM(queries.shape, BF16),
            pltpu.VMEM(new_kv.shape, BF16),
            pltpu.VMEM(gain.shape, BF16),
            pltpu.VMEM((rows, 2, CACHE, KVH * HD), BF16),
            pltpu.SemaphoreType.DMA((4,)),
            pltpu.SemaphoreType.DMA((rows,)),
        ],
        compiler_params=pltpu.CompilerParams(vmem_limit_bytes=16 * 2**20),
        cost_estimate=pl.CostEstimate(flops=10**8, bytes_accessed=3 * 2**20, transcendentals=0),
        name="attend",
    )(*[in_hbm(x) for x in (parents, queries, new_kv, gain, cache_kv)])


def held_shape(gate, features, count):
    return pltpu.VMEM(((count + 1) // 2, gate.shape[0], features * min(count, 2)), BF16)


def column_copies(exchange, owners, gate, up, gate_held, up_held, sems):
    me = lax.axis_index("blk")
    features = gate.shape[1] // exchange.size
    copies = []
    for n, (flip, p) in enumerate(owners):
        device = exchange.device(me, flip, p)
        columns = pl.ds(pl.multiple_of(device * features, features), features)
        place = pl.ds(n % 2 * features, features)
        for k, (source, target) in enumerate(((gate, gate_held), (up, up_held))):
            copies.append(
                pltpu.make_async_copy(source.at[:, columns], target.at[n // 2, :, place], sems.at[2 * n + k])
            )
    return copies


def join_kernel(count, *refs):
    out = refs[-1]
    first = 0
    for part in refs[:count]:
        out[first : first + part.shape[0], :] = part[...]
        first += part.shape[0]


def join(parts, *after):
    rows = sum(p.shape[0] for p in parts)
    return pl.pallas_call(
        functools.partial(join_kernel, len(parts)),
        in_specs=[VMEM] * len(parts) + [ANY] * len(after),
        out_specs=VMEM,
        out_shape=pltpu.VMEM((rows,) + parts[0].shape[1:], parts[0].dtype),
        compiler_params=pltpu.CompilerParams(vmem_limit_bytes=2**20),
        name="join",
    )(*parts, *after)


def load_kernel(exchange, layout, unused, source, out, sems):
    copies = row_copies(exchange, layout, source, out, sems)
    for copy in copies:
        copy.start()
    for copy in copies:
        copy.wait()


def load_first_kernel(exchange, unused, weight, gate, up, weight_out, gate_out, up_out, sem, sems):
    copies = [pltpu.make_async_copy(weight, weight_out, sem)]
    copies += column_copies(exchange, [(0, 0)], gate, up, gate_out, up_out, sems)
    for copy in copies:
        copy.start()
    for copy in copies:
        copy.wait()


def row_copies(exchange, layout, source, out, sems):
    me = lax.axis_index("blk")
    flip, first, count = layout
    rows = source.shape[0] // exchange.size
    copies = []
    for k in range(count):
        device = exchange.device(me, flip, first + k)
        start = pl.multiple_of(device * rows, rows)
        place = pl.ds(k * rows, rows)
        copies.append(pltpu.make_async_copy(source.at[pl.ds(start, rows), :], out.at[place, :], sems.at[k]))
    return copies


def load(exchange, layout, after, source):
    rows = source.shape[0] // exchange.size * layout[2]
    return pl.pallas_call(
        functools.partial(load_kernel, exchange, layout),
        in_specs=[ANY, ANY],
        out_specs=VMEM,
        out_shape=pltpu.VMEM((rows, source.shape[1]), source.dtype),
        scratch_shapes=[pltpu.SemaphoreType.DMA((layout[2],))],
        compiler_params=pltpu.CompilerParams(vmem_limit_bytes=2**20),
        cost_estimate=pl.CostEstimate(flops=0, bytes_accessed=2 * rows * source.shape[1], transcendentals=0),
        name="load",
    )(after, in_hbm(source))


def load_first(exchange, after, weight, gate, up):
    own = held_shape(gate, gate.shape[1] // exchange.size, 1)
    return pl.pallas_call(
        functools.partial(load_first_kernel, exchange),
        in_specs=[ANY] * 4,
        out_specs=[VMEM] * 3,
        out_shape=[pltpu.VMEM(weight.shape, weight.dtype), own, own],
        scratch_shapes=[pltpu.SemaphoreType.DMA, pltpu.SemaphoreType.DMA((2,))],
        compiler_params=pltpu.CompilerParams(vmem_limit_bytes=2**20),
        cost_estimate=pl.CostEstimate(
            flops=0, bytes_accessed=2 * weight.shape[0] * weight.shape[1], transcendentals=0
        ),
        name="load_first",
    )(after, in_hbm(weight), in_hbm(gate), in_hbm(up))


def project_kernel(exchange, layout, fetch, steps, *refs):
    pieces = refs[: len(layout)]
    residual, weight, down, out, copy_out, gains = refs[len(layout) : len(layout) + 6]
    fetched = refs[len(layout) + 6 : len(layout) + 6 + len(fetch)]
    wide, packed, stream, stream_sem, *fetch_sems = refs[len(layout) + 6 + len(fetch) :]
    per_device = wide.shape[0] // exchange.size
    block = per_device + GAIN_ROWS
    beam_rows = out.shape[0]
    step = weight.shape[1] // steps
    stream_copy = pltpu.make_async_copy(residual, stream, stream_sem)
    stream_copy.start()
    fetches = [
        copy
        for rows, target, sems in zip(fetch, fetched, fetch_sems)
        for copy in row_copies(exchange, rows, down, target, sems)
    ]
    for copy in fetches:
        copy.start()

    @apart
    def _():
        me = lax.axis_index("blk")
        for piece, (flip, first, count) in zip(pieces, layout):
            for k in range(count):
                device = exchange.device(me, flip, first + k)
                start = pl.multiple_of(device * per_device, per_device)
                wide[pl.ds(start, per_device), :] = piece[k * block : k * block + per_device, :].astype(F32)
                rows = piece[k * block + per_device : (k + 1) * block, :].astype(F32)
                slot = flip * exchange.half + first + k
                gains[slot : slot + 1, :] = jnp.concatenate(
                    [rows[j : j + 1, :] for j in range(gains.shape[1] // HD)], axis=1
                )
        for h in range(HQ):
            packed[:, h * HD : (h + 1) * HD] = wide[pl.ds(h, beam_rows, stride=HQ), :].astype(BF16)
        summed = None
        for s in range(steps):
            part = slice(s * step, (s + 1) * step)
            term = lax.dot_general(packed[:, part], weight[:, part], NT, preferred_element_type=F32)
            summed = term if summed is None else summed + term
        stream_copy.wait()
        result = (stream[...].astype(F32) + summed).astype(BF16)
        out[...] = result
        copy_out[...] = result
        for copy in fetches:
            copy.wait()


def project(exchange, pieces, residual, weight, down, fetch):
    beam_rows, features = residual.shape
    layout = [p[1:] for p in pieces]
    rows = down.shape[0] // exchange.size
    return pl.pallas_call(
        functools.partial(project_kernel, exchange, layout, fetch, 4),
        in_specs=[VMEM] * len(pieces) + [ANY, VMEM, ANY],
        out_specs=[VMEM] * (3 + len(fetch)),
        out_shape=[
            jax.ShapeDtypeStruct((beam_rows, features), BF16),
            pltpu.VMEM((beam_rows, features), BF16),
            pltpu.VMEM((exchange.size, features), F32),
        ]
        + [pltpu.VMEM((rows * count, down.shape[1]), BF16) for _, _, count in fetch],
        scratch_shapes=[
            pltpu.VMEM((beam_rows * HQ, HD), F32),
            pltpu.VMEM((beam_rows, HQ * HD), BF16),
            pltpu.VMEM((beam_rows, features), BF16),
            pltpu.SemaphoreType.DMA,
        ]
        + [pltpu.SemaphoreType.DMA((count,)) for _, _, count in fetch],
        compiler_params=pltpu.CompilerParams(vmem_limit_bytes=8 * 2**20),
        cost_estimate=pl.CostEstimate(flops=4 * 10**8, bytes_accessed=9 * 2**20, transcendentals=0),
        name="project",
    )(*[p[0] for p in pieces], in_hbm(residual), weight, in_hbm(down))


def enter_kernel(exchange, layout, begun, early, ahead, rows, *refs):
    refs = list(refs)
    take = lambda n: [refs.pop(0) for _ in range(n)]
    blocks = take(len(layout))
    (gains,) = take(1)
    sums = take(3) if begun else None
    early_held = take(2) if early else None
    gate, up = take(2)
    down = take(1)[0] if rows else None
    gate_sum, up_sum, squares = take(3)
    ahead_held = take(2) if ahead else None
    rows_held = take(1)[0] if rows else None
    beam_rows, features = blocks[0].shape[0] // layout[0][2], blocks[0].shape[1]
    owners = [
        (block, k, flip, first + k) for block, (flip, first, count) in zip(blocks, layout) for k in range(count)
    ]
    copies = []
    late_held = None
    if early < len(owners):
        late_held = take(2)
        late = [(flip, p) for _, _, flip, p in owners[early:]]
        copies = column_copies(exchange, late, gate, up, *late_held, refs.pop(0))
    ahead_copies = column_copies(exchange, ahead, gate, up, *ahead_held, refs.pop(0)) if ahead else []
    if rows:
        ahead_copies += row_copies(exchange, rows, down, rows_held, refs.pop(0))
    for copy in copies + ahead_copies:
        copy.start()

    @apart
    def _():
        total = sums[2][...] if begun else jnp.zeros((beam_rows, features), F32)
        for n in range(0, len(owners), 2):
            pair = owners[n : n + 2]
            parts = []
            for block, k, flip, p in pair:
                value = block[k * beam_rows : (k + 1) * beam_rows, :].astype(F32)
                total += value * value
                slot = flip * exchange.half + p
                parts.append((value * gains[slot : slot + 1, :]).astype(BF16))
            normed = jnp.concatenate(parts, axis=1) if len(parts) > 1 else parts[0]
            depth = len(parts) * features
            for which, result in ((0, gate_sum), (1, up_sum)):
                if n < early:
                    held = early_held[which][n // 2, :, :depth]
                else:
                    for m in range(n - early, n - early + len(pair)):
                        copies[2 * m + which].wait()
                    held = late_held[which][(n - early) // 2, :, :depth]
                term = lax.dot_general(normed, held, NT, preferred_element_type=F32)
                if n:
                    result[...] += term
                elif begun:
                    result[...] = sums[which][...] + term
                else:
                    result[...] = term
        squares[...] = total
        for copy in ahead_copies:
            copy.wait()


def enter(exchange, blocks, gains, sums, early_held, gate, up, ahead=(), down=None, rows=None):
    layout = [b[1:] for b in blocks]
    beam_rows, features = blocks[0][0].shape[0] // blocks[0][3], blocks[0][0].shape[1]
    units = gate.shape[0]
    count = sum(b[3] for b in blocks)
    early = 0
    if early_held:
        early = min(count, early_held[0].shape[0] * early_held[0].shape[2] // features)
    late = count - early
    out_shape = [
        pltpu.VMEM((beam_rows, units), F32),
        pltpu.VMEM((beam_rows, units), F32),
        pltpu.VMEM((beam_rows, features), F32),
    ]
    scratch = []
    if late:
        scratch += [held_shape(gate, features, late)] * 2 + [pltpu.SemaphoreType.DMA((2 * late,))]
    if ahead:
        out_shape += [held_shape(gate, features, len(ahead))] * 2
        scratch.append(pltpu.SemaphoreType.DMA((2 * len(ahead),)))
    operands = [b[0] for b in blocks] + [gains] + list(sums or ()) + list(early_held or ())
    operands += [in_hbm(gate), in_hbm(up)]
    in_specs = [VMEM] * (len(operands) - 2) + [ANY] * 2
    if rows:
        operands.append(in_hbm(down))
        in_specs.append(ANY)
        out_shape.append(pltpu.VMEM((down.shape[0] // exchange.size * rows[2], units), BF16))
        scratch.append(pltpu.SemaphoreType.DMA((rows[2],)))
    return pl.pallas_call(
        functools.partial(enter_kernel, exchange, layout, sums is not None, early, ahead, rows),
        in_specs=in_specs,
        out_specs=[VMEM] * len(out_shape),
        out_shape=out_shape,
        scratch_shapes=scratch,
        compiler_params=pltpu.CompilerParams(
            vmem_limit_bytes=(late + late % 2) * 4 * units * features + 2 * 2**20
        ),
        cost_estimate=pl.CostEstimate(
            flops=count * 4 * beam_rows * units * features,
            bytes_accessed=count * 4 * units * features,
            transcendentals=0,
        ),
        name="enter",
    )(*operands)


def leave_kernel(first, *refs):
    if first:
        gate_sum, up_sum, squares, down, out, hidden = refs
        mean = jnp.sum(squares[...], axis=1, keepdims=True) / D
        inverse_rms = lax.rsqrt(mean + epsilon)
        hidden[...] = (jax.nn.silu(gate_sum[...] * inverse_rms) * (up_sum[...] * inverse_rms)).astype(BF16)
    else:
        hidden, down, *_, out = refs
    count, _, features = out.shape
    wide = 2 if count % 2 == 0 else 1
    for n in range(0, count, wide):
        term = lax.dot_general(
            hidden[...], down[n * features : (n + wide) * features, :], NT, preferred_element_type=F32
        )
        for j in range(wide):
            out[n + j] = term[:, j * features : (j + 1) * features].astype(out.dtype)


def leave(inputs, down, features, dtype, *after):
    first = len(inputs) == 3
    beam_rows, units = inputs[0].shape
    count = down.shape[0] // features
    out_shape = [pltpu.VMEM((count, beam_rows, features), dtype)]
    if first:
        out_shape.append(pltpu.VMEM((beam_rows, units), BF16))
    results = pl.pallas_call(
        functools.partial(leave_kernel, first),
        in_specs=[VMEM] * (len(inputs) + 1) + [ANY] * len(after),
        out_specs=[VMEM] * len(out_shape),
        out_shape=out_shape,
        compiler_params=pltpu.CompilerParams(vmem_limit_bytes=4 * 2**20),
        cost_estimate=pl.CostEstimate(flops=0, bytes_accessed=2**10, transcendentals=0),
        name="leave",
    )(*inputs, down, *after)
    return results if first else results[0]


def fast_shards(size, queries, new_kv, cache_kv, parents, residual, out_proj, norm_gain, w_gate, w_up, w_down):
    exchange = Exchange(size)
    features = residual.shape[0]
    high, low = (4, 4), (0, 4)

    mixed = attend(parents, queries, new_kv, cache_kv, norm_gain)
    fresh = exchange.swap(mixed, 0)
    high_send = load(exchange, (1,) + high, mixed, w_down)
    have = join([mixed, fresh], high_send)
    fresh = exchange.swap(have, 1)
    high_keep = load(exchange, (0,) + high, have, w_down)
    have = join([have, fresh], high_keep)
    other = exchange.swap_core(have)
    fresh = exchange.swap(have, 2)
    weight, *held = load_first(exchange, have, out_proj, w_gate, w_up)
    fresh = join([fresh], weight, other)
    pieces = [(have, 0, 0, 4), (other, 1, 0, 4), (fresh, 0, 4, 4), (exchange.swap_core(fresh), 1, 4, 4)]
    after, have, gains, low_send = project(exchange, pieces, residual.T, weight, w_down, [(1,) + low])

    block0 = have
    other0 = exchange.swap_core(block0)
    fresh1 = exchange.swap(block0, 0)
    *sums, g, u = enter(exchange, [(block0, 0, 0, 1)], gains, None, held, w_gate, w_up, [(0, 1), (1, 0)])
    have = join([block0, fresh1], sums[2], other0)
    other1 = exchange.swap_core(fresh1)
    fresh2 = exchange.swap(have, 1)
    *sums, g, u = enter(
        exchange, [(fresh1, 0, 1, 1), (other0, 1, 0, 1)], gains, sums, [g, u], w_gate, w_up, [(0, 2), (0, 3)]
    )
    have = join([have, fresh2], sums[2], other1)
    other2 = exchange.swap_core(fresh2)
    fresh3 = exchange.swap(have, 2)
    *sums, g, u = enter(
        exchange,
        [(fresh2, 0, 2, 2), (other1, 1, 1, 1)],
        gains, sums, [g, u], w_gate, w_up, [(1, 2), (1, 3), (0, 4), (0, 5)],
    )
    fresh3 = join([fresh3], sums[2], other2)
    other3 = exchange.swap_core(fresh3)
    last = [(1, 4), (1, 5), (1, 6), (1, 7)]
    *sums, g, u = enter(
        exchange, [(other2, 1, 2, 2), (fresh3, 0, 4, 4)], gains, sums, [g, u], w_gate, w_up, last
    )
    *sums, low_keep = enter(
        exchange, [(other3, 1, 4, 4)], gains, sums, [g, u], w_gate, w_up, (), w_down, (0,) + low
    )

    send, hidden = leave(sums, high_send, features, BF16)
    received = exchange.swap_core(send).astype(F32)
    keep = leave((hidden,), high_keep, features, F32, send)
    onward = (keep + received).astype(BF16)
    passed = exchange.swap(onward, 2)
    send = leave((hidden,), low_send, features, BF16, onward)
    received = exchange.swap_core(send).astype(F32)
    keep = leave((hidden,), low_keep, features, F32, send)
    keep = keep + received + passed.astype(F32)
    for stage in (1, 0):
        part = keep.shape[0] // 2
        keep = keep[:part] + exchange.swap(keep[part:].astype(BF16), stage).astype(F32)
    layer_out = (after.astype(F32) + keep[0]).astype(BF16)
    return (after.T, layer_out.T)


def solution(mesh):
    size = mesh.shape["blk"]

    def shards(*args):
        features, beam_rows = args[4].shape
        units = args[7].shape[0]
        fits = (
            size == 16
            and features % HD == 0
            and features // HD <= GAIN_ROWS
            and beam_rows % 16 == 0
            and beam_rows * HQ * HD <= 2**20
            and units % HD == 0
            and units * features <= 2**20
        )
        return functools.partial(fast_shards, size)(*args) if fits else plain_shards(*args)

    return jax.shard_map(
        shards,
        mesh=mesh,
        in_specs=(
            P(("groups", "blk"), None),
            P(("groups", "blk"), None, None),
            P(("groups", "blk"), None, None, None),
            P(("groups", "blk")),
            P("blk", "groups"),
            P("blk", None),
            P("blk"),
            P("blk", None),
            P("blk", None),
            P(None, "blk"),
        ),
        out_specs=(P("blk", "groups"), P("blk", "groups")),
        check_vma=False,
    )
```

```python
import functools
import math

import jax
import jax.numpy as jnp
from jax import lax
from jax.experimental import pallas as pl
from jax.experimental.pallas import tpu as pltpu
from jax.sharding import PartitionSpec as P

D = 8192
HQ = 64
KVH = 8
HD = 128
CACHE = 256
GAIN_ROWS = 16

epsilon = 1e-06
F32 = jnp.float32
BF16 = jnp.bfloat16
NT = (((1,), (1,)), ((), ()))
VMEM = pl.BlockSpec(memory_space=pltpu.VMEM)
ANY = pl.BlockSpec(memory_space=pl.ANY)
SMEM = pl.BlockSpec(memory_space=pltpu.SMEM)


def attend_rows(queries, new_kv, cache_kv, parents):
    row_count = queries.shape[0]
    group_size = HQ // KVH
    local_parent = parents - lax.axis_index("blk") * row_count
    chosen = jnp.take(cache_kv, local_parent, axis=0)
    cache_keys = chosen[:, 0].reshape(row_count, CACHE, KVH, HD)
    cache_values = chosen[:, 1].reshape(row_count, CACHE, KVH, HD)
    new_key = new_kv[:, 0].reshape(row_count, KVH, HD)
    new_value = new_kv[:, 1].reshape(row_count, KVH, HD)
    query_heads = queries.reshape(row_count, KVH, group_size, HD)
    score_scale = 1.0 / math.sqrt(HD)
    score_cache = (
        jnp.einsum("rgjd,rcgd->rgjc", query_heads, cache_keys, preferred_element_type=jnp.float32)
        * score_scale
    )
    score_new = (
        jnp.einsum("rgjd,rgd->rgj", query_heads, new_key, preferred_element_type=jnp.float32)
        * score_scale
    )
    score_top = jnp.maximum(jnp.max(score_cache, axis=-1), score_new)
    expo_cache = jnp.exp(score_cache - score_top[..., None])
    expo_new = jnp.exp(score_new - score_top)
    denom_sum = jnp.sum(expo_cache, axis=-1) + expo_new
    weight_cache = (expo_cache / denom_sum[..., None]).astype(jnp.bfloat16)
    weight_new = (expo_new / denom_sum).astype(jnp.bfloat16)
    mixed_heads = jnp.einsum(
        "rgjc,rcgd->rgjd", weight_cache, cache_values, preferred_element_type=jnp.float32
    )
    mixed_heads = (
        mixed_heads
        + weight_new.astype(jnp.float32)[..., None] * new_value.astype(jnp.float32)[:, :, None, :]
    )
    return mixed_heads.reshape(row_count, HQ * HD).astype(jnp.bfloat16)


def plain_shards(queries, new_kv, cache_kv, parents, residual, out_proj, norm_gain, w_gate, w_up, w_down):
    attended = attend_rows(queries, new_kv, cache_kv, parents)
    projected = lax.dot_general(
        out_proj,
        lax.all_gather(attended, "blk", axis=0, tiled=True),
        (((1,), (1,)), ((), ())),
        preferred_element_type=jnp.float32,
    )
    after_attention = (residual.astype(jnp.float32) + projected).astype(jnp.bfloat16)
    widened = after_attention.astype(jnp.float32)
    gathered, gain_all = (
        lax.all_gather(after_attention, "blk", axis=0, tiled=True),
        lax.all_gather(norm_gain, "blk", axis=0, tiled=True),
    )
    gathered_wide = gathered.astype(jnp.float32)
    inverse_rms = lax.rsqrt(jnp.sum(gathered_wide * gathered_wide, axis=0) / D + epsilon)
    normed_all = (
        gathered_wide * inverse_rms[None, :] * gain_all.astype(jnp.float32)[:, None]
    ).astype(jnp.bfloat16)
    gate_sum = jnp.dot(w_gate, normed_all, preferred_element_type=jnp.float32)
    up_sum = jnp.dot(w_up, normed_all, preferred_element_type=jnp.float32)
    hidden = (jax.nn.silu(gate_sum) * up_sum).astype(jnp.bfloat16)
    ffn_delta = lax.psum_scatter(
        jnp.dot(w_down, hidden, preferred_element_type=jnp.float32),
        "blk",
        scatter_dimension=0,
        tiled=True,
    )
    layer_out = (widened + ffn_delta).astype(jnp.bfloat16)
    return (after_attention, layer_out)


class Exchange:
    def __init__(self, size):
        self.size = size
        bits = size.bit_length() - 1
        down = [1 << b for b in range(bits - 1, 0, -1)]
        other = list(down)
        if len(other) > 1:
            other[-1], other[-2] = other[-2], other[-1]
        self.masks = (other, down)
        self.half = size // 2

    def offset(self, core, p):
        return sum(m for k, m in enumerate(self.masks[core]) if p >> k & 1)

    def device(self, me, flip, p):
        core = (me & 1) ^ flip
        return (me ^ flip) ^ jnp.where(core == 1, self.offset(1, p), self.offset(0, p))

    def swap(self, x, stage):
        pairs = [(i, i ^ self.masks[i & 1][stage]) for i in range(self.size)]
        return lax.ppermute(x, "blk", pairs)

    def swap_core(self, x):
        return lax.ppermute(x, "blk", [(i, i ^ 1) for i in range(self.size)])


def apart(body):
    pl.when(lax.axis_index("blk") >= 0)(body)


def attend_kernel(parents, queries, new_kv, gain, cache, out, chosen, asked, fresh, scaling, held, small_sems, sems):
    rows = held.shape[0]
    base = lax.axis_index("blk") * rows
    others = [
        pltpu.make_async_copy(source, target, small_sems.at[k])
        for k, (source, target) in enumerate([(parents, chosen), (queries, asked), (new_kv, fresh), (gain, scaling)])
    ]
    copies = [pltpu.make_async_copy(cache.at[r], held.at[r], sems.at[r]) for r in range(rows)]
    for copy in others + copies:
        copy.start()
    scale = 1.0 / math.sqrt(HD)
    group = HQ // KVH
    width = KVH * HD

    @apart
    def _():
        head = lax.broadcasted_iota(jnp.int32, (HQ, width), 0) // group
        column = lax.broadcasted_iota(jnp.int32, (HQ, width), 1) // HD
        own = head == column
        for copy in others:
            copy.wait()
        gain_rows = scaling.shape[0]
        out[rows * HQ :, :] = jnp.concatenate(
            [scaling[...].astype(F32), jnp.zeros((GAIN_ROWS - gain_rows, HD), F32)], axis=0
        ).astype(BF16)
        for copy in copies:
            copy.wait()
        for r in range(rows):
            parent = chosen[r] - base
            query = asked[:, r, :].astype(F32)
            spread = jnp.where(own, jnp.concatenate([query] * KVH, axis=1), 0.0)
            new_key = fresh[r, 0:1, :].astype(F32)
            new_value = fresh[r, 1:2, :].astype(F32)
            score_new = jnp.sum(spread * new_key, axis=1, keepdims=True) * scale
            keys = held[parent, 0]
            values = held[parent, 1]
            score = lax.dot_general(spread.astype(BF16), keys, NT, preferred_element_type=F32) * scale
            top = jnp.maximum(jnp.max(score, axis=1, keepdims=True), score_new)
            expo = jnp.exp(score - top)
            expo_new = jnp.exp(score_new - top)
            total = jnp.sum(expo, axis=1, keepdims=True) + expo_new
            weight = (expo / total).astype(BF16)
            weight_new = (expo_new / total).astype(BF16).astype(F32)
            mixed = jnp.dot(weight, values, preferred_element_type=F32) + weight_new * new_value
            out[r * HQ : (r + 1) * HQ, :] = jnp.concatenate(
                [mixed[g * group : (g + 1) * group, g * HD : (g + 1) * HD] for g in range(KVH)], axis=0
            ).astype(BF16)


def in_hbm(x):
    return pltpu.with_memory_space_constraint(x, pltpu.HBM)


def attend(parents, queries, new_kv, cache_kv, norm_gain):
    rows = queries.shape[0]
    gain = norm_gain.reshape(-1, HD)
    queries = queries.reshape(rows, HQ, HD).transpose(1, 0, 2)
    return pl.pallas_call(
        attend_kernel,
        in_specs=[ANY] * 5,
        out_specs=VMEM,
        out_shape=pltpu.VMEM((rows * HQ + GAIN_ROWS, HD), BF16),
        scratch_shapes=[
            pltpu.SMEM(parents.shape, parents.dtype),
            pltpu.VMEM(queries.shape, BF16),
            pltpu.VMEM(new_kv.shape, BF16),
            pltpu.VMEM(gain.shape, BF16),
            pltpu.VMEM((rows, 2, CACHE, KVH * HD), BF16),
            pltpu.SemaphoreType.DMA((4,)),
            pltpu.SemaphoreType.DMA((rows,)),
        ],
        compiler_params=pltpu.CompilerParams(vmem_limit_bytes=16 * 2**20),
        cost_estimate=pl.CostEstimate(flops=10**8, bytes_accessed=3 * 2**20, transcendentals=0),
        name="attend",
    )(*[in_hbm(x) for x in (parents, queries, new_kv, gain, cache_kv)])


def held_shape(gate, features, count):
    return pltpu.VMEM(((count + 1) // 2, gate.shape[0], features * min(count, 2)), BF16)


def column_copies(exchange, owners, gate, up, gate_held, up_held, sems):
    me = lax.axis_index("blk")
    features = gate.shape[1] // exchange.size
    copies = []
    for n, (flip, p) in enumerate(owners):
        device = exchange.device(me, flip, p)
        columns = pl.ds(pl.multiple_of(device * features, features), features)
        place = pl.ds(n % 2 * features, features)
        for k, (source, target) in enumerate(((gate, gate_held), (up, up_held))):
            copies.append(
                pltpu.make_async_copy(source.at[:, columns], target.at[n // 2, :, place], sems.at[2 * n + k])
            )
    return copies


def join_kernel(count, *refs):
    out = refs[-1]
    first = 0
    for part in refs[:count]:
        out[first : first + part.shape[0], :] = part[...]
        first += part.shape[0]


def join(parts, *after):
    rows = sum(p.shape[0] for p in parts)
    return pl.pallas_call(
        functools.partial(join_kernel, len(parts)),
        in_specs=[VMEM] * len(parts) + [ANY] * len(after),
        out_specs=VMEM,
        out_shape=pltpu.VMEM((rows,) + parts[0].shape[1:], parts[0].dtype),
        compiler_params=pltpu.CompilerParams(vmem_limit_bytes=2**20),
        name="join",
    )(*parts, *after)


def load_kernel(exchange, layout, unused, source, out, sems):
    copies = row_copies(exchange, layout, source, out, sems)
    for copy in copies:
        copy.start()
    for copy in copies:
        copy.wait()


def load_first_kernel(exchange, unused, weight, gate, up, weight_out, gate_out, up_out, sem, sems):
    copies = [pltpu.make_async_copy(weight, weight_out, sem)]
    copies += column_copies(exchange, [(0, 0)], gate, up, gate_out, up_out, sems)
    for copy in copies:
        copy.start()
    for copy in copies:
        copy.wait()


def row_copies(exchange, layout, source, out, sems):
    me = lax.axis_index("blk")
    flip, first, count = layout
    rows = source.shape[0] // exchange.size
    copies = []
    for k in range(count):
        device = exchange.device(me, flip, first + k)
        start = pl.multiple_of(device * rows, rows)
        place = pl.ds(k * rows, rows)
        copies.append(pltpu.make_async_copy(source.at[pl.ds(start, rows), :], out.at[place, :], sems.at[k]))
    return copies


def load(exchange, layout, after, source):
    rows = source.shape[0] // exchange.size * layout[2]
    return pl.pallas_call(
        functools.partial(load_kernel, exchange, layout),
        in_specs=[ANY, ANY],
        out_specs=VMEM,
        out_shape=pltpu.VMEM((rows, source.shape[1]), source.dtype),
        scratch_shapes=[pltpu.SemaphoreType.DMA((layout[2],))],
        compiler_params=pltpu.CompilerParams(vmem_limit_bytes=2**20),
        cost_estimate=pl.CostEstimate(flops=0, bytes_accessed=2 * rows * source.shape[1], transcendentals=0),
        name="load",
    )(after, in_hbm(source))


def load_columns_kernel(exchange, owners, unused, gate, up, gate_out, up_out, sems):
    copies = column_copies(exchange, owners, gate, up, gate_out, up_out, sems)
    for copy in copies:
        copy.start()
    for copy in copies:
        copy.wait()


def load_columns(exchange, owners, after, gate, up):
    held = held_shape(gate, gate.shape[1] // exchange.size, len(owners))
    return pl.pallas_call(
        functools.partial(load_columns_kernel, exchange, owners),
        in_specs=[ANY] * 3,
        out_specs=[VMEM] * 2,
        out_shape=[held, held],
        scratch_shapes=[pltpu.SemaphoreType.DMA((2 * len(owners),))],
        compiler_params=pltpu.CompilerParams(vmem_limit_bytes=2**20),
        cost_estimate=pl.CostEstimate(flops=0, bytes_accessed=5 * 2**20, transcendentals=0),
        name="load_columns",
    )(after, in_hbm(gate), in_hbm(up))


def load_first(exchange, after, weight, gate, up):
    own = held_shape(gate, gate.shape[1] // exchange.size, 1)
    return pl.pallas_call(
        functools.partial(load_first_kernel, exchange),
        in_specs=[ANY] * 4,
        out_specs=[VMEM] * 3,
        out_shape=[pltpu.VMEM(weight.shape, weight.dtype), own, own],
        scratch_shapes=[pltpu.SemaphoreType.DMA, pltpu.SemaphoreType.DMA((2,))],
        compiler_params=pltpu.CompilerParams(vmem_limit_bytes=2**20),
        cost_estimate=pl.CostEstimate(
            flops=0, bytes_accessed=2 * weight.shape[0] * weight.shape[1], transcendentals=0
        ),
        name="load_first",
    )(after, in_hbm(weight), in_hbm(gate), in_hbm(up))


def project_kernel(exchange, layout, fetch, owners, steps, *refs):
    pieces = refs[: len(layout)]
    residual, weight, down, gate, up, out, copy_out, gains, fetched, gate_out, up_out = refs[len(layout) :][:11]
    wide, packed, stream, stream_sem, fetch_sems, ahead_sems = refs[len(layout) :][11:]
    per_device = wide.shape[0] // exchange.size
    block = per_device + GAIN_ROWS
    beam_rows = out.shape[0]
    step = weight.shape[1] // steps
    stream_copy = pltpu.make_async_copy(residual, stream, stream_sem)
    stream_copy.start()
    fetches = row_copies(exchange, fetch, down, fetched, fetch_sems)
    fetches += column_copies(exchange, owners, gate, up, gate_out, up_out, ahead_sems)
    for copy in fetches:
        copy.start()

    @apart
    def _():
        me = lax.axis_index("blk")
        for piece, (flip, first, count) in zip(pieces, layout):
            for k in range(count):
                device = exchange.device(me, flip, first + k)
                start = pl.multiple_of(device * per_device, per_device)
                wide[pl.ds(start, per_device), :] = piece[k * block : k * block + per_device, :].astype(F32)
                rows = piece[k * block + per_device : (k + 1) * block, :].astype(F32)
                slot = flip * exchange.half + first + k
                gains[slot : slot + 1, :] = jnp.concatenate(
                    [rows[j : j + 1, :] for j in range(gains.shape[1] // HD)], axis=1
                )
        for h in range(HQ):
            packed[:, h * HD : (h + 1) * HD] = wide[pl.ds(h, beam_rows, stride=HQ), :].astype(BF16)
        summed = None
        for s in range(steps):
            part = slice(s * step, (s + 1) * step)
            term = lax.dot_general(packed[:, part], weight[:, part], NT, preferred_element_type=F32)
            summed = term if summed is None else summed + term
        stream_copy.wait()
        result = (stream[...].astype(F32) + summed).astype(BF16)
        out[...] = result
        copy_out[...] = result
        for copy in fetches:
            copy.wait()


def project(exchange, pieces, residual, weight, down, fetch, gate, up, owners):
    beam_rows, features = residual.shape
    layout = [p[1:] for p in pieces]
    rows = down.shape[0] // exchange.size
    return pl.pallas_call(
        functools.partial(project_kernel, exchange, layout, fetch, owners, 4),
        in_specs=[VMEM] * len(pieces) + [ANY, VMEM, ANY, ANY, ANY],
        out_specs=[VMEM] * 6,
        out_shape=[
            jax.ShapeDtypeStruct((beam_rows, features), BF16),
            pltpu.VMEM((beam_rows, features), BF16),
            pltpu.VMEM((exchange.size, features), F32),
            pltpu.VMEM((rows * fetch[2], down.shape[1]), BF16),
            held_shape(gate, features, len(owners)),
            held_shape(gate, features, len(owners)),
        ],
        scratch_shapes=[
            pltpu.VMEM((beam_rows * HQ, HD), F32),
            pltpu.VMEM((beam_rows, HQ * HD), BF16),
            pltpu.VMEM((beam_rows, features), BF16),
            pltpu.SemaphoreType.DMA,
            pltpu.SemaphoreType.DMA((fetch[2],)),
            pltpu.SemaphoreType.DMA((2 * len(owners),)),
        ],
        compiler_params=pltpu.CompilerParams(vmem_limit_bytes=8 * 2**20),
        cost_estimate=pl.CostEstimate(flops=4 * 10**8, bytes_accessed=9 * 2**20, transcendentals=0),
        name="project",
    )(*[p[0] for p in pieces], in_hbm(residual), weight, in_hbm(down), in_hbm(gate), in_hbm(up))


def enter_kernel(exchange, layout, begun, groups, ahead, rows, *refs):
    refs = list(refs)
    take = lambda n: [refs.pop(0) for _ in range(n)]
    blocks = take(len(layout))
    (gains,) = take(1)
    sums = take(3) if begun else None
    held = [take(2) for _ in groups]
    gate, up = take(2)
    down = take(1)[0] if rows else None
    gate_sum, up_sum, squares = take(3)
    beam_rows, features = blocks[0].shape[0] // layout[0][2], blocks[0].shape[1]
    owners = [
        (block, k, flip, first + k) for block, (flip, first, count) in zip(blocks, layout) for k in range(count)
    ]
    chunks = []
    for pair, count in zip(held, groups):
        for n in range(0, count, 2):
            chunks.append((pair, n // 2, [owners.pop(0) for _ in range(min(2, count - n))]))
    copies = column_copies(exchange, ahead, gate, up, *refs) if ahead else []
    if rows:
        copies = row_copies(exchange, rows, down, *refs)
    for copy in copies:
        copy.start()

    @apart
    def _():
        total = sums[2][...] if begun else jnp.zeros((beam_rows, features), F32)
        for c, (pair, slot, members) in enumerate(chunks):
            parts = []
            for block, k, flip, p in members:
                value = block[k * beam_rows : (k + 1) * beam_rows, :].astype(F32)
                total += value * value
                row = flip * exchange.half + p
                parts.append((value * gains[row : row + 1, :]).astype(BF16))
            normed = jnp.concatenate(parts, axis=1) if len(parts) > 1 else parts[0]
            depth = len(parts) * features
            for which, result in ((0, gate_sum), (1, up_sum)):
                term = lax.dot_general(normed, pair[which][slot, :, :depth], NT, preferred_element_type=F32)
                if c:
                    result[...] += term
                elif begun:
                    result[...] = sums[which][...] + term
                else:
                    result[...] = term
        squares[...] = total
        for copy in copies:
            copy.wait()


def enter(exchange, blocks, gains, sums, held, gate, up, ahead=(), down=None, rows=None):
    layout = [b[1:] for b in blocks]
    beam_rows, features = blocks[0][0].shape[0] // blocks[0][3], blocks[0][0].shape[1]
    units = gate.shape[0]
    count = sum(b[3] for b in blocks)
    out_shape = [
        pltpu.VMEM((beam_rows, units), F32),
        pltpu.VMEM((beam_rows, units), F32),
        pltpu.VMEM((beam_rows, features), F32),
    ]
    scratch = []
    if ahead:
        out_shape += [held_shape(gate, features, len(ahead))] * 2
        scratch.append(pltpu.SemaphoreType.DMA((2 * len(ahead),)))
    operands = [b[0] for b in blocks] + [gains] + list(sums or ()) + [x for h in held for x in h[:2]]
    in_specs = [VMEM] * len(operands) + [ANY] * 2
    operands += [in_hbm(gate), in_hbm(up)]
    if rows:
        operands.append(in_hbm(down))
        in_specs.append(ANY)
        out_shape.append(pltpu.VMEM((down.shape[0] // exchange.size * rows[2], units), BF16))
        scratch.append(pltpu.SemaphoreType.DMA((rows[2],)))
    return pl.pallas_call(
        functools.partial(enter_kernel, exchange, layout, sums is not None, [h[2] for h in held], ahead, rows),
        in_specs=in_specs,
        out_specs=[VMEM] * len(out_shape),
        out_shape=out_shape,
        scratch_shapes=scratch,
        compiler_params=pltpu.CompilerParams(vmem_limit_bytes=4 * 2**20),
        cost_estimate=pl.CostEstimate(
            flops=count * 4 * beam_rows * units * features,
            bytes_accessed=count * 4 * units * features,
            transcendentals=0,
        ),
        name="enter",
    )(*operands)


def leave_kernel(first, *refs):
    if first:
        gate_sum, up_sum, squares, down, out, hidden = refs
        mean = jnp.sum(squares[...], axis=1, keepdims=True) / D
        inverse_rms = lax.rsqrt(mean + epsilon)
        hidden[...] = (jax.nn.silu(gate_sum[...] * inverse_rms) * (up_sum[...] * inverse_rms)).astype(BF16)
    else:
        hidden, down, *_, out = refs
    count, _, features = out.shape
    wide = 2 if count % 2 == 0 else 1
    for n in range(0, count, wide):
        term = lax.dot_general(
            hidden[...], down[n * features : (n + wide) * features, :], NT, preferred_element_type=F32
        )
        for j in range(wide):
            out[n + j] = term[:, j * features : (j + 1) * features].astype(out.dtype)


def leave(inputs, down, features, dtype, *after):
    first = len(inputs) == 3
    beam_rows, units = inputs[0].shape
    count = down.shape[0] // features
    out_shape = [pltpu.VMEM((count, beam_rows, features), dtype)]
    if first:
        out_shape.append(pltpu.VMEM((beam_rows, units), BF16))
    results = pl.pallas_call(
        functools.partial(leave_kernel, first),
        in_specs=[VMEM] * (len(inputs) + 1) + [ANY] * len(after),
        out_specs=[VMEM] * len(out_shape),
        out_shape=out_shape,
        compiler_params=pltpu.CompilerParams(vmem_limit_bytes=4 * 2**20),
        cost_estimate=pl.CostEstimate(flops=0, bytes_accessed=2**10, transcendentals=0),
        name="leave",
    )(*inputs, down, *after)
    return results if first else results[0]


def leave_low_kernel(exchange, rows, hidden, down_send, down, unused, send, keep, held, sems):
    copies = row_copies(exchange, rows, down, held, sems)
    for copy in copies:
        copy.start()
    count, _, features = send.shape

    @apart
    def _():
        for held_rows, out in ((down_send, send), (held, keep)):
            for n in range(0, count, 2):
                if out is keep:
                    copies[n].wait()
                    copies[n + 1].wait()
                term = lax.dot_general(
                    hidden[...], held_rows[n * features : (n + 2) * features, :], NT, preferred_element_type=F32
                )
                for j in range(2):
                    out[n + j] = term[:, j * features : (j + 1) * features].astype(out.dtype)


def leave_low(exchange, hidden, down_send, down, rows, after):
    beam_rows, units = hidden.shape
    count = rows[2]
    features = down_send.shape[0] // count
    return pl.pallas_call(
        functools.partial(leave_low_kernel, exchange, rows),
        in_specs=[VMEM, VMEM, ANY, ANY],
        out_specs=[VMEM, VMEM],
        out_shape=[
            pltpu.VMEM((count, beam_rows, features), BF16),
            pltpu.VMEM((count, beam_rows, features), F32),
        ],
        scratch_shapes=[pltpu.VMEM(down_send.shape, BF16), pltpu.SemaphoreType.DMA((count,))],
        compiler_params=pltpu.CompilerParams(vmem_limit_bytes=12 * 2**20),
        cost_estimate=pl.CostEstimate(flops=0, bytes_accessed=2**10, transcendentals=0),
        name="leave_low",
    )(hidden, down_send, in_hbm(down), after)


def fold_kernel(kept, passed, out):
    out[...] = kept[...] + passed[...].astype(F32)


def fold(kept, passed):
    return pl.pallas_call(
        fold_kernel,
        in_specs=[VMEM] * 2,
        out_specs=VMEM,
        out_shape=pltpu.VMEM(kept.shape, F32),
        compiler_params=pltpu.CompilerParams(vmem_limit_bytes=2**20),
        name="fold",
    )(kept, passed)


def fast_shards(size, queries, new_kv, cache_kv, parents, residual, out_proj, norm_gain, w_gate, w_up, w_down):
    exchange = Exchange(size)
    features = residual.shape[0]
    high, low = (4, 4), (0, 4)

    mixed = attend(parents, queries, new_kv, cache_kv, norm_gain)
    fresh = exchange.swap(mixed, 0)
    high_send = load(exchange, (1,) + high, mixed, w_down)
    have = join([mixed, fresh], high_send)
    fresh = exchange.swap(have, 1)
    held1 = load_columns(exchange, [(0, 1), (1, 0)], have, w_gate, w_up)
    have = join([have, fresh], held1[0])
    other = exchange.swap_core(have)
    fresh = exchange.swap(have, 2)
    weight, *held0 = load_first(exchange, have, out_proj, w_gate, w_up)
    fresh = join([fresh], weight, other)
    pieces = [(have, 0, 0, 4), (other, 1, 0, 4), (fresh, 0, 4, 4), (exchange.swap_core(fresh), 1, 4, 4)]
    after, have, gains, low_send, *held3 = project(
        exchange, pieces, residual.T, weight, w_down, (1,) + low, w_gate, w_up, [(1, 1)]
    )

    block0 = have
    other0 = exchange.swap_core(block0)
    fresh1 = exchange.swap(block0, 0)
    *sums, g, u = enter(
        exchange, [(block0, 0, 0, 1)], gains, None, [(*held0, 1)], w_gate, w_up, [(0, 2), (0, 3)]
    )
    held2 = (g, u, 2)
    have = join([block0, fresh1], sums[2], other0)
    other1 = exchange.swap_core(fresh1)
    fresh2 = exchange.swap(have, 1)
    *sums, g, u = enter(
        exchange, [(fresh1, 0, 1, 1), (other0, 1, 0, 1)], gains, sums, [(*held1, 2)], w_gate, w_up, [(1, 2), (1, 3)]
    )
    held4 = (g, u, 2)
    have = join([have, fresh2], sums[2], other1)
    other2 = exchange.swap_core(fresh2)
    fresh3 = exchange.swap(have, 2)
    *sums, g, u = enter(
        exchange,
        [(fresh2, 0, 2, 2), (other1, 1, 1, 1)],
        gains, sums, [held2, (*held3, 1)], w_gate, w_up, [(0, 4), (0, 5), (0, 6), (0, 7)],
    )
    held5 = (g, u, 4)
    fresh3 = join([fresh3], sums[2], other2)
    other3 = exchange.swap_core(fresh3)
    *sums, g, u = enter(
        exchange,
        [(other2, 1, 2, 2), (fresh3, 0, 4, 4)],
        gains, sums, [held4, held5], w_gate, w_up, [(1, 4), (1, 5), (1, 6), (1, 7)],
    )
    *sums, high_keep = enter(
        exchange, [(other3, 1, 4, 4)], gains, sums, [(g, u, 4)], w_gate, w_up, (), w_down, (0,) + high
    )

    send, hidden = leave(sums, high_send, features, BF16)
    received = exchange.swap_core(send).astype(F32)
    keep = leave((hidden,), high_keep, features, F32, send)
    onward = (keep + received).astype(BF16)
    passed = exchange.swap(onward, 2)
    send, keep = leave_low(exchange, hidden, low_send, w_down, (0,) + low, onward)
    received = exchange.swap_core(send).astype(F32)
    keep = fold(keep, passed) + received
    for stage in (1, 0):
        part = keep.shape[0] // 2
        keep = keep[:part] + exchange.swap(keep[part:].astype(BF16), stage).astype(F32)
    layer_out = (after.astype(F32) + keep[0]).astype(BF16)
    return (after.T, layer_out.T)


def solution(mesh):
    size = mesh.shape["blk"]

    def shards(*args):
        features, beam_rows = args[4].shape
        units = args[7].shape[0]
        fits = (
            size == 16
            and features % HD == 0
            and features // HD <= GAIN_ROWS
            and beam_rows % 16 == 0
            and beam_rows * HQ * HD <= 2**20
            and units % HD == 0
            and units * features <= 2**20
        )
        return functools.partial(fast_shards, size)(*args) if fits else plain_shards(*args)

    return jax.shard_map(
        shards,
        mesh=mesh,
        in_specs=(
            P(("groups", "blk"), None),
            P(("groups", "blk"), None, None),
            P(("groups", "blk"), None, None, None),
            P(("groups", "blk")),
            P("blk", "groups"),
            P("blk", None),
            P("blk"),
            P("blk", None),
            P("blk", None),
            P(None, "blk"),
        ),
        out_specs=(P("blk", "groups"), P("blk", "groups")),
        check_vma=False,
    )
```

```python
import functools
import math

import jax
import jax.numpy as jnp
from jax import lax
from jax.experimental import pallas as pl
from jax.experimental.pallas import tpu as pltpu
from jax.sharding import PartitionSpec as P

D = 8192
HQ = 64
KVH = 8
HD = 128
CACHE = 256
GAIN_ROWS = 16

epsilon = 1e-06
F32 = jnp.float32
BF16 = jnp.bfloat16
NT = (((1,), (1,)), ((), ()))
VMEM = pl.BlockSpec(memory_space=pltpu.VMEM)
ANY = pl.BlockSpec(memory_space=pl.ANY)
SMEM = pl.BlockSpec(memory_space=pltpu.SMEM)


def attend_rows(queries, new_kv, cache_kv, parents):
    row_count = queries.shape[0]
    group_size = HQ // KVH
    local_parent = parents - lax.axis_index("blk") * row_count
    chosen = jnp.take(cache_kv, local_parent, axis=0)
    cache_keys = chosen[:, 0].reshape(row_count, CACHE, KVH, HD)
    cache_values = chosen[:, 1].reshape(row_count, CACHE, KVH, HD)
    new_key = new_kv[:, 0].reshape(row_count, KVH, HD)
    new_value = new_kv[:, 1].reshape(row_count, KVH, HD)
    query_heads = queries.reshape(row_count, KVH, group_size, HD)
    score_scale = 1.0 / math.sqrt(HD)
    score_cache = (
        jnp.einsum("rgjd,rcgd->rgjc", query_heads, cache_keys, preferred_element_type=jnp.float32)
        * score_scale
    )
    score_new = (
        jnp.einsum("rgjd,rgd->rgj", query_heads, new_key, preferred_element_type=jnp.float32)
        * score_scale
    )
    score_top = jnp.maximum(jnp.max(score_cache, axis=-1), score_new)
    expo_cache = jnp.exp(score_cache - score_top[..., None])
    expo_new = jnp.exp(score_new - score_top)
    denom_sum = jnp.sum(expo_cache, axis=-1) + expo_new
    weight_cache = (expo_cache / denom_sum[..., None]).astype(jnp.bfloat16)
    weight_new = (expo_new / denom_sum).astype(jnp.bfloat16)
    mixed_heads = jnp.einsum(
        "rgjc,rcgd->rgjd", weight_cache, cache_values, preferred_element_type=jnp.float32
    )
    mixed_heads = (
        mixed_heads
        + weight_new.astype(jnp.float32)[..., None] * new_value.astype(jnp.float32)[:, :, None, :]
    )
    return mixed_heads.reshape(row_count, HQ * HD).astype(jnp.bfloat16)


def plain_shards(queries, new_kv, cache_kv, parents, residual, out_proj, norm_gain, w_gate, w_up, w_down):
    attended = attend_rows(queries, new_kv, cache_kv, parents)
    projected = lax.dot_general(
        out_proj,
        lax.all_gather(attended, "blk", axis=0, tiled=True),
        (((1,), (1,)), ((), ())),
        preferred_element_type=jnp.float32,
    )
    after_attention = (residual.astype(jnp.float32) + projected).astype(jnp.bfloat16)
    widened = after_attention.astype(jnp.float32)
    gathered, gain_all = (
        lax.all_gather(after_attention, "blk", axis=0, tiled=True),
        lax.all_gather(norm_gain, "blk", axis=0, tiled=True),
    )
    gathered_wide = gathered.astype(jnp.float32)
    inverse_rms = lax.rsqrt(jnp.sum(gathered_wide * gathered_wide, axis=0) / D + epsilon)
    normed_all = (
        gathered_wide * inverse_rms[None, :] * gain_all.astype(jnp.float32)[:, None]
    ).astype(jnp.bfloat16)
    gate_sum = jnp.dot(w_gate, normed_all, preferred_element_type=jnp.float32)
    up_sum = jnp.dot(w_up, normed_all, preferred_element_type=jnp.float32)
    hidden = (jax.nn.silu(gate_sum) * up_sum).astype(jnp.bfloat16)
    ffn_delta = lax.psum_scatter(
        jnp.dot(w_down, hidden, preferred_element_type=jnp.float32),
        "blk",
        scatter_dimension=0,
        tiled=True,
    )
    layer_out = (widened + ffn_delta).astype(jnp.bfloat16)
    return (after_attention, layer_out)


class Exchange:
    def __init__(self, size):
        self.size = size
        bits = size.bit_length() - 1
        down = [1 << b for b in range(bits - 1, 0, -1)]
        other = list(down)
        if len(other) > 1:
            other[-1], other[-2] = other[-2], other[-1]
        self.masks = (other, down)
        self.half = size // 2

    def offset(self, core, p):
        return sum(m for k, m in enumerate(self.masks[core]) if p >> k & 1)

    def device(self, me, flip, p):
        core = (me & 1) ^ flip
        return (me ^ flip) ^ jnp.where(core == 1, self.offset(1, p), self.offset(0, p))

    def swap(self, x, stage):
        pairs = [(i, i ^ self.masks[i & 1][stage]) for i in range(self.size)]
        return lax.ppermute(x, "blk", pairs)

    def swap_core(self, x):
        return lax.ppermute(x, "blk", [(i, i ^ 1) for i in range(self.size)])


def apart(body):
    pl.when(lax.axis_index("blk") >= 0)(body)


def attend_kernel(parents, queries, new_kv, gain, cache, out, chosen, asked, fresh, scaling, held, small_sems, sems):
    rows = held.shape[0]
    base = lax.axis_index("blk") * rows
    others = [
        pltpu.make_async_copy(source, target, small_sems.at[k])
        for k, (source, target) in enumerate([(parents, chosen), (queries, asked), (new_kv, fresh), (gain, scaling)])
    ]
    copies = [
        pltpu.make_async_copy(cache.at[r, k], held.at[r, k], sems.at[k, r]) for k in range(2) for r in range(rows)
    ]
    for copy in others + copies:
        copy.start()
    scale = 1.0 / math.sqrt(HD)
    group = HQ // KVH
    width = KVH * HD

    @apart
    def _():
        head = lax.broadcasted_iota(jnp.int32, (HQ, width), 0) // group
        column = lax.broadcasted_iota(jnp.int32, (HQ, width), 1) // HD
        own = head == column
        for copy in others:
            copy.wait()
        gain_rows = scaling.shape[0]
        out[rows * HQ :, :] = jnp.concatenate(
            [scaling[...].astype(F32), jnp.zeros((GAIN_ROWS - gain_rows, HD), F32)], axis=0
        ).astype(BF16)
        for copy in copies[:rows]:
            copy.wait()
        weights = []
        for r in range(rows):
            query = asked[:, r, :].astype(F32)
            spread = jnp.where(own, jnp.concatenate([query] * KVH, axis=1), 0.0)
            new_key = fresh[r, 0:1, :].astype(F32)
            score_new = jnp.sum(spread * new_key, axis=1, keepdims=True) * scale
            keys = held[chosen[r] - base, 0]
            score = lax.dot_general(spread.astype(BF16), keys, NT, preferred_element_type=F32) * scale
            top = jnp.maximum(jnp.max(score, axis=1, keepdims=True), score_new)
            expo = jnp.exp(score - top)
            expo_new = jnp.exp(score_new - top)
            total = jnp.sum(expo, axis=1, keepdims=True) + expo_new
            weights.append(((expo / total).astype(BF16), (expo_new / total).astype(BF16).astype(F32)))
        for copy in copies[rows:]:
            copy.wait()
        for r, (weight, weight_new) in enumerate(weights):
            new_value = fresh[r, 1:2, :].astype(F32)
            values = held[chosen[r] - base, 1]
            mixed = jnp.dot(weight, values, preferred_element_type=F32) + weight_new * new_value
            out[r * HQ : (r + 1) * HQ, :] = jnp.concatenate(
                [mixed[g * group : (g + 1) * group, g * HD : (g + 1) * HD] for g in range(KVH)], axis=0
            ).astype(BF16)


def in_hbm(x):
    return pltpu.with_memory_space_constraint(x, pltpu.HBM)


def attend(parents, queries, new_kv, cache_kv, norm_gain):
    rows = queries.shape[0]
    gain = norm_gain.reshape(-1, HD)
    queries = queries.reshape(rows, HQ, HD).transpose(1, 0, 2)
    return pl.pallas_call(
        attend_kernel,
        in_specs=[ANY] * 5,
        out_specs=VMEM,
        out_shape=pltpu.VMEM((rows * HQ + GAIN_ROWS, HD), BF16),
        scratch_shapes=[
            pltpu.SMEM(parents.shape, parents.dtype),
            pltpu.VMEM(queries.shape, BF16),
            pltpu.VMEM(new_kv.shape, BF16),
            pltpu.VMEM(gain.shape, BF16),
            pltpu.VMEM((rows, 2, CACHE, KVH * HD), BF16),
            pltpu.SemaphoreType.DMA((4,)),
            pltpu.SemaphoreType.DMA((2, rows)),
        ],
        compiler_params=pltpu.CompilerParams(vmem_limit_bytes=16 * 2**20),
        cost_estimate=pl.CostEstimate(flops=10**8, bytes_accessed=3 * 2**20, transcendentals=0),
        name="attend",
    )(*[in_hbm(x) for x in (parents, queries, new_kv, gain, cache_kv)])


def beside(count):
    return 4 if count % 4 == 0 else min(count, 2)


def held_shape(gate, features, count):
    wide = beside(count)
    return pltpu.VMEM((count // wide, gate.shape[0], features * wide), BF16)


def column_copies(exchange, owners, gate, up, gate_held, up_held, sems):
    me = lax.axis_index("blk")
    features = gate.shape[1] // exchange.size
    wide = beside(len(owners))
    copies = []
    for n, (flip, p) in enumerate(owners):
        device = exchange.device(me, flip, p)
        columns = pl.ds(pl.multiple_of(device * features, features), features)
        place = pl.ds(n % wide * features, features)
        for k, (source, target) in enumerate(((gate, gate_held), (up, up_held))):
            copies.append(
                pltpu.make_async_copy(source.at[:, columns], target.at[n // wide, :, place], sems.at[2 * n + k])
            )
    return copies


def join_kernel(count, *refs):
    out = refs[-1]
    first = 0
    for part in refs[:count]:
        out[first : first + part.shape[0], :] = part[...]
        first += part.shape[0]


def join(parts, *after):
    rows = sum(p.shape[0] for p in parts)
    return pl.pallas_call(
        functools.partial(join_kernel, len(parts)),
        in_specs=[VMEM] * len(parts) + [ANY] * len(after),
        out_specs=VMEM,
        out_shape=pltpu.VMEM((rows,) + parts[0].shape[1:], parts[0].dtype),
        compiler_params=pltpu.CompilerParams(vmem_limit_bytes=2**20),
        name="join",
    )(*parts, *after)


def load_kernel(exchange, layout, unused, source, out, sems):
    copies = row_copies(exchange, layout, source, out, sems)
    for copy in copies:
        copy.start()
    for copy in copies:
        copy.wait()


def load_first_kernel(exchange, unused, weight, gate, up, weight_out, gate_out, up_out, sem, sems):
    copies = [pltpu.make_async_copy(weight, weight_out, sem)]
    copies += column_copies(exchange, [(0, 0)], gate, up, gate_out, up_out, sems)
    for copy in copies:
        copy.start()
    for copy in copies:
        copy.wait()


def row_copies(exchange, layout, source, out, sems):
    me = lax.axis_index("blk")
    flip, first, count = layout
    rows = source.shape[0] // exchange.size
    copies = []
    for k in range(count):
        device = exchange.device(me, flip, first + k)
        start = pl.multiple_of(device * rows, rows)
        place = pl.ds(k * rows, rows)
        copies.append(pltpu.make_async_copy(source.at[pl.ds(start, rows), :], out.at[place, :], sems.at[k]))
    return copies


def load(exchange, layout, after, source):
    rows = source.shape[0] // exchange.size * layout[2]
    return pl.pallas_call(
        functools.partial(load_kernel, exchange, layout),
        in_specs=[ANY, ANY],
        out_specs=VMEM,
        out_shape=pltpu.VMEM((rows, source.shape[1]), source.dtype),
        scratch_shapes=[pltpu.SemaphoreType.DMA((layout[2],))],
        compiler_params=pltpu.CompilerParams(vmem_limit_bytes=2**20),
        cost_estimate=pl.CostEstimate(flops=0, bytes_accessed=2 * rows * source.shape[1], transcendentals=0),
        name="load",
    )(after, in_hbm(source))


def load_columns_kernel(exchange, owners, unused, gate, up, gate_out, up_out, sems):
    copies = column_copies(exchange, owners, gate, up, gate_out, up_out, sems)
    for copy in copies:
        copy.start()
    for copy in copies:
        copy.wait()


def load_columns(exchange, owners, after, gate, up):
    held = held_shape(gate, gate.shape[1] // exchange.size, len(owners))
    return pl.pallas_call(
        functools.partial(load_columns_kernel, exchange, owners),
        in_specs=[ANY] * 3,
        out_specs=[VMEM] * 2,
        out_shape=[held, held],
        scratch_shapes=[pltpu.SemaphoreType.DMA((2 * len(owners),))],
        compiler_params=pltpu.CompilerParams(vmem_limit_bytes=2**20),
        cost_estimate=pl.CostEstimate(flops=0, bytes_accessed=5 * 2**20, transcendentals=0),
        name="load_columns",
    )(after, in_hbm(gate), in_hbm(up))


def load_first(exchange, after, weight, gate, up):
    own = held_shape(gate, gate.shape[1] // exchange.size, 1)
    return pl.pallas_call(
        functools.partial(load_first_kernel, exchange),
        in_specs=[ANY] * 4,
        out_specs=[VMEM] * 3,
        out_shape=[pltpu.VMEM(weight.shape, weight.dtype), own, own],
        scratch_shapes=[pltpu.SemaphoreType.DMA, pltpu.SemaphoreType.DMA((2,))],
        compiler_params=pltpu.CompilerParams(vmem_limit_bytes=2**20),
        cost_estimate=pl.CostEstimate(
            flops=0, bytes_accessed=2 * weight.shape[0] * weight.shape[1], transcendentals=0
        ),
        name="load_first",
    )(after, in_hbm(weight), in_hbm(gate), in_hbm(up))


def project_kernel(exchange, layout, owners, steps, *refs):
    pieces = refs[: len(layout)]
    residual, weight, gate, up, out, copy_out, gains, gate_out, up_out = refs[len(layout) :][:9]
    wide, packed, stream, stream_sem, ahead_sems = refs[len(layout) :][9:]
    per_device = wide.shape[0] // exchange.size
    block = per_device + GAIN_ROWS
    beam_rows = out.shape[0]
    step = weight.shape[1] // steps
    stream_copy = pltpu.make_async_copy(residual, stream, stream_sem)
    stream_copy.start()
    fetches = column_copies(exchange, owners, gate, up, gate_out, up_out, ahead_sems)
    for copy in fetches:
        copy.start()

    @apart
    def _():
        me = lax.axis_index("blk")
        for piece, (flip, first, count) in zip(pieces, layout):
            for k in range(count):
                device = exchange.device(me, flip, first + k)
                start = pl.multiple_of(device * per_device, per_device)
                wide[pl.ds(start, per_device), :] = piece[k * block : k * block + per_device, :].astype(F32)
                rows = piece[k * block + per_device : (k + 1) * block, :].astype(F32)
                slot = flip * exchange.half + first + k
                gains[slot : slot + 1, :] = jnp.concatenate(
                    [rows[j : j + 1, :] for j in range(gains.shape[1] // HD)], axis=1
                )
        for h in range(HQ):
            packed[:, h * HD : (h + 1) * HD] = wide[pl.ds(h, beam_rows, stride=HQ), :].astype(BF16)
        summed = None
        for s in range(steps):
            part = slice(s * step, (s + 1) * step)
            term = lax.dot_general(packed[:, part], weight[:, part], NT, preferred_element_type=F32)
            summed = term if summed is None else summed + term
        stream_copy.wait()
        result = (stream[...].astype(F32) + summed).astype(BF16)
        out[...] = result
        copy_out[...] = result
        for copy in fetches:
            copy.wait()


def project(exchange, pieces, residual, weight, gate, up, owners):
    beam_rows, features = residual.shape
    layout = [p[1:] for p in pieces]
    return pl.pallas_call(
        functools.partial(project_kernel, exchange, layout, owners, 4),
        in_specs=[VMEM] * len(pieces) + [ANY, VMEM, ANY, ANY],
        out_specs=[VMEM] * 5,
        out_shape=[
            jax.ShapeDtypeStruct((beam_rows, features), BF16),
            pltpu.VMEM((beam_rows, features), BF16),
            pltpu.VMEM((exchange.size, features), F32),
            held_shape(gate, features, len(owners)),
            held_shape(gate, features, len(owners)),
        ],
        scratch_shapes=[
            pltpu.VMEM((beam_rows * HQ, HD), F32),
            pltpu.VMEM((beam_rows, HQ * HD), BF16),
            pltpu.VMEM((beam_rows, features), BF16),
            pltpu.SemaphoreType.DMA,
            pltpu.SemaphoreType.DMA((2 * len(owners),)),
        ],
        compiler_params=pltpu.CompilerParams(vmem_limit_bytes=8 * 2**20),
        cost_estimate=pl.CostEstimate(flops=4 * 10**8, bytes_accessed=9 * 2**20, transcendentals=0),
        name="project",
    )(*[p[0] for p in pieces], in_hbm(residual), weight, in_hbm(gate), in_hbm(up))


def enter_kernel(exchange, layout, begun, groups, ahead, rows, *refs):
    refs = list(refs)
    take = lambda n: [refs.pop(0) for _ in range(n)]
    blocks = take(len(layout))
    (gains,) = take(1)
    sums = take(3) if begun else None
    held = [take(2) for _ in groups]
    gate, up = take(2)
    down = take(1)[0] if rows else None
    gate_sum, up_sum, squares = take(3)
    beam_rows, features = blocks[0].shape[0] // layout[0][2], blocks[0].shape[1]
    owners = [
        (block, k, flip, first + k) for block, (flip, first, count) in zip(blocks, layout) for k in range(count)
    ]
    chunks = []
    for pair, count in zip(held, groups):
        wide = beside(count)
        for n in range(count // wide):
            chunks.append((pair, n, [owners.pop(0) for _ in range(wide)]))
    copies = column_copies(exchange, ahead, gate, up, *refs) if ahead else []
    if rows:
        copies = row_copies(exchange, rows, down, *refs)
    for copy in copies:
        copy.start()

    @apart
    def _():
        total = sums[2][...] if begun else jnp.zeros((beam_rows, features), F32)
        for c, (pair, slot, members) in enumerate(chunks):
            parts = []
            for block, k, flip, p in members:
                value = block[k * beam_rows : (k + 1) * beam_rows, :].astype(F32)
                total += value * value
                row = flip * exchange.half + p
                parts.append((value * gains[row : row + 1, :]).astype(BF16))
            normed = jnp.concatenate(parts, axis=1) if len(parts) > 1 else parts[0]
            depth = len(parts) * features
            for which, result in ((0, gate_sum), (1, up_sum)):
                term = lax.dot_general(normed, pair[which][slot, :, :depth], NT, preferred_element_type=F32)
                if c:
                    result[...] += term
                elif begun:
                    result[...] = sums[which][...] + term
                else:
                    result[...] = term
        squares[...] = total
        for copy in copies:
            copy.wait()


def enter(exchange, blocks, gains, sums, held, gate, up, ahead=(), down=None, rows=None):
    layout = [b[1:] for b in blocks]
    beam_rows, features = blocks[0][0].shape[0] // blocks[0][3], blocks[0][0].shape[1]
    units = gate.shape[0]
    count = sum(b[3] for b in blocks)
    out_shape = [
        pltpu.VMEM((beam_rows, units), F32),
        pltpu.VMEM((beam_rows, units), F32),
        pltpu.VMEM((beam_rows, features), F32),
    ]
    scratch = []
    if ahead:
        out_shape += [held_shape(gate, features, len(ahead))] * 2
        scratch.append(pltpu.SemaphoreType.DMA((2 * len(ahead),)))
    operands = [b[0] for b in blocks] + [gains] + list(sums or ()) + [x for h in held for x in h[:2]]
    in_specs = [VMEM] * len(operands) + [ANY] * 2
    operands += [in_hbm(gate), in_hbm(up)]
    if rows:
        operands.append(in_hbm(down))
        in_specs.append(ANY)
        out_shape.append(pltpu.VMEM((down.shape[0] // exchange.size * rows[2], units), BF16))
        scratch.append(pltpu.SemaphoreType.DMA((rows[2],)))
    return pl.pallas_call(
        functools.partial(enter_kernel, exchange, layout, sums is not None, [h[2] for h in held], ahead, rows),
        in_specs=in_specs,
        out_specs=[VMEM] * len(out_shape),
        out_shape=out_shape,
        scratch_shapes=scratch,
        compiler_params=pltpu.CompilerParams(vmem_limit_bytes=4 * 2**20),
        cost_estimate=pl.CostEstimate(
            flops=count * 4 * beam_rows * units * features,
            bytes_accessed=count * 4 * units * features,
            transcendentals=0,
        ),
        name="enter",
    )(*operands)


def leave_kernel(exchange, first, rows, *refs):
    refs = list(refs)
    take = lambda n: [refs.pop(0) for _ in range(n)]
    inputs = take(3 if first else 1)
    held, down, _ = take(3)
    (out,) = take(1)
    hidden = take(1)[0] if first else inputs[0]
    copies = row_copies(exchange, rows, down, *refs)
    for copy in copies:
        copy.start()

    @apart
    def _():
        if first:
            gate_sum, up_sum, squares = inputs
            mean = jnp.sum(squares[...], axis=1, keepdims=True) / D
            inverse_rms = lax.rsqrt(mean + epsilon)
            hidden[...] = (jax.nn.silu(gate_sum[...] * inverse_rms) * (up_sum[...] * inverse_rms)).astype(BF16)
        count, _, features = out.shape
        wide = beside(count)
        for n in range(0, count, wide):
            term = lax.dot_general(
                hidden[...], held[n * features : (n + wide) * features, :], NT, preferred_element_type=F32
            )
            for j in range(wide):
                out[n + j] = term[:, j * features : (j + 1) * features].astype(out.dtype)
        for copy in copies:
            copy.wait()


def leave(exchange, inputs, held, features, dtype, down, rows, after):
    first = len(inputs) == 3
    beam_rows, units = inputs[0].shape
    count = held.shape[0] // features
    out_shape = [pltpu.VMEM((count, beam_rows, features), dtype)]
    if first:
        out_shape.append(pltpu.VMEM((beam_rows, units), BF16))
    out_shape.append(pltpu.VMEM((rows[2] * features, units), BF16))
    return pl.pallas_call(
        functools.partial(leave_kernel, exchange, first, rows),
        in_specs=[VMEM] * (len(inputs) + 1) + [ANY] * 2,
        out_specs=[VMEM] * len(out_shape),
        out_shape=out_shape,
        scratch_shapes=[pltpu.SemaphoreType.DMA((rows[2],))],
        compiler_params=pltpu.CompilerParams(vmem_limit_bytes=4 * 2**20),
        cost_estimate=pl.CostEstimate(flops=0, bytes_accessed=2**10, transcendentals=0),
        name="leave",
    )(*inputs, held, in_hbm(down), after)


def leave_low_kernel(exchange, rows, hidden, send_one, send_two, down, unused, send, keep, held, sems):
    copies = row_copies(exchange, rows, down, held, sems)
    for copy in copies:
        copy.start()
    count, _, features = send.shape

    @apart
    def _():
        for out in (send, keep):
            for n in range(0, count, 2):
                if out is keep:
                    copies[n].wait()
                    copies[n + 1].wait()
                    part = held[n * features : (n + 2) * features, :]
                else:
                    part = (send_one, send_two)[n // 2][...]
                term = lax.dot_general(hidden[...], part, NT, preferred_element_type=F32)
                for j in range(2):
                    out[n + j] = term[:, j * features : (j + 1) * features].astype(out.dtype)


def leave_low(exchange, hidden, send_one, send_two, down, rows, after):
    beam_rows, units = hidden.shape
    count = rows[2]
    features = send_one.shape[0] // 2
    return pl.pallas_call(
        functools.partial(leave_low_kernel, exchange, rows),
        in_specs=[VMEM, VMEM, VMEM, ANY, ANY],
        out_specs=[VMEM, VMEM],
        out_shape=[
            pltpu.VMEM((count, beam_rows, features), BF16),
            pltpu.VMEM((count, beam_rows, features), F32),
        ],
        scratch_shapes=[pltpu.VMEM((count * features, units), BF16), pltpu.SemaphoreType.DMA((count,))],
        compiler_params=pltpu.CompilerParams(vmem_limit_bytes=12 * 2**20),
        cost_estimate=pl.CostEstimate(flops=0, bytes_accessed=2**10, transcendentals=0),
        name="leave_low",
    )(hidden, send_one, send_two, in_hbm(down), after)


def fold_kernel(kept, passed, out):
    out[...] = kept[...] + passed[...].astype(F32)


def fold(kept, passed):
    return pl.pallas_call(
        fold_kernel,
        in_specs=[VMEM] * 2,
        out_specs=VMEM,
        out_shape=pltpu.VMEM(kept.shape, F32),
        compiler_params=pltpu.CompilerParams(vmem_limit_bytes=2**20),
        name="fold",
    )(kept, passed)


def fast_shards(size, queries, new_kv, cache_kv, parents, residual, out_proj, norm_gain, w_gate, w_up, w_down):
    exchange = Exchange(size)
    features = residual.shape[0]
    high, low = (4, 4), (0, 4)

    mixed = attend(parents, queries, new_kv, cache_kv, norm_gain)
    fresh = exchange.swap(mixed, 0)
    high_send = load(exchange, (1,) + high, mixed, w_down)
    have = join([mixed, fresh], high_send)
    fresh = exchange.swap(have, 1)
    held3 = load_columns(exchange, [(1, 0), (1, 1)], have, w_gate, w_up)
    have = join([have, fresh], held3[0])
    other = exchange.swap_core(have)
    fresh = exchange.swap(have, 2)
    weight, *held0 = load_first(exchange, have, out_proj, w_gate, w_up)
    fresh = join([fresh], weight, other)
    pieces = [(have, 0, 0, 4), (other, 1, 0, 4), (fresh, 0, 4, 4), (exchange.swap_core(fresh), 1, 4, 4)]
    after, have, gains, *held1 = project(exchange, pieces, residual.T, weight, w_gate, w_up, [(0, 1)])

    block0 = have
    fresh1 = exchange.swap(block0, 0)
    *sums, g, u = enter(
        exchange, [(block0, 0, 0, 1)], gains, None, [(*held0, 1)], w_gate, w_up, [(0, 2), (0, 3)]
    )
    held2 = (g, u, 2)
    have = join([block0, fresh1], sums[2])
    other1 = exchange.swap_core(have)
    fresh2 = exchange.swap(have, 1)
    *sums, g, u = enter(
        exchange, [(fresh1, 0, 1, 1)], gains, sums, [(*held1, 1)], w_gate, w_up, [(1, 2), (1, 3)]
    )
    held4 = (g, u, 2)
    have = join([have, fresh2], sums[2], other1)
    other2 = exchange.swap_core(fresh2)
    fresh3 = exchange.swap(have, 2)
    *sums, g, u = enter(
        exchange,
        [(fresh2, 0, 2, 2), (other1, 1, 0, 2)],
        gains, sums, [held2, (*held3, 2)], w_gate, w_up, [(0, 4), (0, 5), (0, 6), (0, 7)],
    )
    held5 = (g, u, 4)
    fresh3 = join([fresh3], sums[2], other2)
    other3 = exchange.swap_core(fresh3)
    *sums, g, u = enter(
        exchange,
        [(other2, 1, 2, 2), (fresh3, 0, 4, 4)],
        gains, sums, [held4, held5], w_gate, w_up, [(1, 4), (1, 5), (1, 6), (1, 7)],
    )
    *sums, high_keep = enter(
        exchange, [(other3, 1, 4, 4)], gains, sums, [(g, u, 4)], w_gate, w_up, (), w_down, (0,) + high
    )

    send, hidden, low_one = leave(exchange, sums, high_send, features, BF16, w_down, (1, 0, 2), sums[2])
    received = exchange.swap_core(send).astype(F32)
    keep, low_two = leave(exchange, (hidden,), high_keep, features, F32, w_down, (1, 2, 2), send)
    onward = (keep + received).astype(BF16)
    passed = exchange.swap(onward, 2)
    send, keep = leave_low(exchange, hidden, low_one, low_two, w_down, (0,) + low, onward)
    received = exchange.swap_core(send).astype(F32)
    keep = fold(keep, passed) + received
    for stage in (1, 0):
        part = keep.shape[0] // 2
        keep = keep[:part] + exchange.swap(keep[part:].astype(BF16), stage).astype(F32)
    layer_out = (after.astype(F32) + keep[0]).astype(BF16)
    return (after.T, layer_out.T)


def solution(mesh):
    size = mesh.shape["blk"]

    def shards(*args):
        features, beam_rows = args[4].shape
        units = args[7].shape[0]
        fits = (
            size == 16
            and features % HD == 0
            and features // HD <= GAIN_ROWS
            and beam_rows % 16 == 0
            and beam_rows * HQ * HD <= 2**20
            and units % HD == 0
            and units * features <= 2**20
        )
        return functools.partial(fast_shards, size)(*args) if fits else plain_shards(*args)

    return jax.shard_map(
        shards,
        mesh=mesh,
        in_specs=(
            P(("groups", "blk"), None),
            P(("groups", "blk"), None, None),
            P(("groups", "blk"), None, None, None),
            P(("groups", "blk")),
            P("blk", "groups"),
            P("blk", None),
            P("blk"),
            P("blk", None),
            P("blk", None),
            P(None, "blk"),
        ),
        out_specs=(P("blk", "groups"), P("blk", "groups")),
        check_vma=False,
    )
```

```python
import functools
import math

import jax
import jax.numpy as jnp
from jax import lax
from jax.experimental import pallas as pl
from jax.experimental.pallas import tpu as pltpu
from jax.sharding import PartitionSpec as P

D = 8192
HQ = 64
KVH = 8
HD = 128
CACHE = 256
GAIN_ROWS = 16

epsilon = 1e-06
F32 = jnp.float32
BF16 = jnp.bfloat16
NT = (((1,), (1,)), ((), ()))
VMEM = pl.BlockSpec(memory_space=pltpu.VMEM)
ANY = pl.BlockSpec(memory_space=pl.ANY)
SMEM = pl.BlockSpec(memory_space=pltpu.SMEM)


def attend_rows(queries, new_kv, cache_kv, parents):
    row_count = queries.shape[0]
    group_size = HQ // KVH
    local_parent = parents - lax.axis_index("blk") * row_count
    chosen = jnp.take(cache_kv, local_parent, axis=0)
    cache_keys = chosen[:, 0].reshape(row_count, CACHE, KVH, HD)
    cache_values = chosen[:, 1].reshape(row_count, CACHE, KVH, HD)
    new_key = new_kv[:, 0].reshape(row_count, KVH, HD)
    new_value = new_kv[:, 1].reshape(row_count, KVH, HD)
    query_heads = queries.reshape(row_count, KVH, group_size, HD)
    score_scale = 1.0 / math.sqrt(HD)
    score_cache = (
        jnp.einsum("rgjd,rcgd->rgjc", query_heads, cache_keys, preferred_element_type=jnp.float32)
        * score_scale
    )
    score_new = (
        jnp.einsum("rgjd,rgd->rgj", query_heads, new_key, preferred_element_type=jnp.float32)
        * score_scale
    )
    score_top = jnp.maximum(jnp.max(score_cache, axis=-1), score_new)
    expo_cache = jnp.exp(score_cache - score_top[..., None])
    expo_new = jnp.exp(score_new - score_top)
    denom_sum = jnp.sum(expo_cache, axis=-1) + expo_new
    weight_cache = (expo_cache / denom_sum[..., None]).astype(jnp.bfloat16)
    weight_new = (expo_new / denom_sum).astype(jnp.bfloat16)
    mixed_heads = jnp.einsum(
        "rgjc,rcgd->rgjd", weight_cache, cache_values, preferred_element_type=jnp.float32
    )
    mixed_heads = (
        mixed_heads
        + weight_new.astype(jnp.float32)[..., None] * new_value.astype(jnp.float32)[:, :, None, :]
    )
    return mixed_heads.reshape(row_count, HQ * HD).astype(jnp.bfloat16)


def plain_shards(queries, new_kv, cache_kv, parents, residual, out_proj, norm_gain, w_gate, w_up, w_down):
    attended = attend_rows(queries, new_kv, cache_kv, parents)
    projected = lax.dot_general(
        out_proj,
        lax.all_gather(attended, "blk", axis=0, tiled=True),
        (((1,), (1,)), ((), ())),
        preferred_element_type=jnp.float32,
    )
    after_attention = (residual.astype(jnp.float32) + projected).astype(jnp.bfloat16)
    widened = after_attention.astype(jnp.float32)
    gathered, gain_all = (
        lax.all_gather(after_attention, "blk", axis=0, tiled=True),
        lax.all_gather(norm_gain, "blk", axis=0, tiled=True),
    )
    gathered_wide = gathered.astype(jnp.float32)
    inverse_rms = lax.rsqrt(jnp.sum(gathered_wide * gathered_wide, axis=0) / D + epsilon)
    normed_all = (
        gathered_wide * inverse_rms[None, :] * gain_all.astype(jnp.float32)[:, None]
    ).astype(jnp.bfloat16)
    gate_sum = jnp.dot(w_gate, normed_all, preferred_element_type=jnp.float32)
    up_sum = jnp.dot(w_up, normed_all, preferred_element_type=jnp.float32)
    hidden = (jax.nn.silu(gate_sum) * up_sum).astype(jnp.bfloat16)
    ffn_delta = lax.psum_scatter(
        jnp.dot(w_down, hidden, preferred_element_type=jnp.float32),
        "blk",
        scatter_dimension=0,
        tiled=True,
    )
    layer_out = (widened + ffn_delta).astype(jnp.bfloat16)
    return (after_attention, layer_out)


class Exchange:
    def __init__(self, size):
        self.size = size
        bits = size.bit_length() - 1
        down = [1 << b for b in range(bits - 1, 0, -1)]
        other = list(down)
        if len(other) > 1:
            other[-1], other[-2] = other[-2], other[-1]
        self.masks = (other, down)
        self.half = size // 2

    def offset(self, core, p):
        return sum(m for k, m in enumerate(self.masks[core]) if p >> k & 1)

    def device(self, me, flip, p):
        core = (me & 1) ^ flip
        return (me ^ flip) ^ jnp.where(core == 1, self.offset(1, p), self.offset(0, p))

    def swap(self, x, stage):
        pairs = [(i, i ^ self.masks[i & 1][stage]) for i in range(self.size)]
        return lax.ppermute(x, "blk", pairs)

    def swap_core(self, x):
        return lax.ppermute(x, "blk", [(i, i ^ 1) for i in range(self.size)])


def apart(body):
    pl.when(lax.axis_index("blk") >= 0)(body)


def attend_kernel(parents, queries, new_kv, gain, cache, out, chosen, asked, fresh, scaling, held, small_sems, sems):
    rows = held.shape[0]
    base = lax.axis_index("blk") * rows
    others = [
        pltpu.make_async_copy(source, target, small_sems.at[k])
        for k, (source, target) in enumerate([(parents, chosen), (queries, asked), (new_kv, fresh), (gain, scaling)])
    ]
    copies = [
        pltpu.make_async_copy(cache.at[r, k], held.at[r, k], sems.at[k, r]) for k in range(2) for r in range(rows)
    ]
    for copy in others + copies:
        copy.start()
    scale = 1.0 / math.sqrt(HD)
    group = HQ // KVH
    width = KVH * HD

    @apart
    def _():
        head = lax.broadcasted_iota(jnp.int32, (HQ, width), 0) // group
        column = lax.broadcasted_iota(jnp.int32, (HQ, width), 1) // HD
        own = head == column
        for copy in others:
            copy.wait()
        gain_rows = scaling.shape[0]
        out[rows * HQ :, :] = jnp.concatenate(
            [scaling[...].astype(F32), jnp.zeros((GAIN_ROWS - gain_rows, HD), F32)], axis=0
        ).astype(BF16)
        for copy in copies[:rows]:
            copy.wait()
        weights = []
        for r in range(rows):
            query = asked[:, r, :].astype(F32)
            spread = jnp.where(own, jnp.concatenate([query] * KVH, axis=1), 0.0)
            new_key = fresh[r, 0:1, :].astype(F32)
            score_new = jnp.sum(spread * new_key, axis=1, keepdims=True) * scale
            keys = held[chosen[r] - base, 0]
            score = lax.dot_general(spread.astype(BF16), keys, NT, preferred_element_type=F32) * scale
            top = jnp.maximum(jnp.max(score, axis=1, keepdims=True), score_new)
            expo = jnp.exp(score - top)
            expo_new = jnp.exp(score_new - top)
            total = jnp.sum(expo, axis=1, keepdims=True) + expo_new
            weights.append(((expo / total).astype(BF16), (expo_new / total).astype(BF16).astype(F32)))
        for copy in copies[rows:]:
            copy.wait()
        for r, (weight, weight_new) in enumerate(weights):
            new_value = fresh[r, 1:2, :].astype(F32)
            values = held[chosen[r] - base, 1]
            mixed = jnp.dot(weight, values, preferred_element_type=F32) + weight_new * new_value
            out[r * HQ : (r + 1) * HQ, :] = jnp.concatenate(
                [mixed[g * group : (g + 1) * group, g * HD : (g + 1) * HD] for g in range(KVH)], axis=0
            ).astype(BF16)


def in_hbm(x):
    return pltpu.with_memory_space_constraint(x, pltpu.HBM)


def attend(parents, queries, new_kv, cache_kv, norm_gain):
    rows = queries.shape[0]
    gain = norm_gain.reshape(-1, HD)
    queries = queries.reshape(rows, HQ, HD).transpose(1, 0, 2)
    return pl.pallas_call(
        attend_kernel,
        in_specs=[ANY] * 5,
        out_specs=VMEM,
        out_shape=pltpu.VMEM((rows * HQ + GAIN_ROWS, HD), BF16),
        scratch_shapes=[
            pltpu.SMEM(parents.shape, parents.dtype),
            pltpu.VMEM(queries.shape, BF16),
            pltpu.VMEM(new_kv.shape, BF16),
            pltpu.VMEM(gain.shape, BF16),
            pltpu.VMEM((rows, 2, CACHE, KVH * HD), BF16),
            pltpu.SemaphoreType.DMA((4,)),
            pltpu.SemaphoreType.DMA((2, rows)),
        ],
        compiler_params=pltpu.CompilerParams(vmem_limit_bytes=16 * 2**20),
        cost_estimate=pl.CostEstimate(flops=10**8, bytes_accessed=3 * 2**20, transcendentals=0),
        name="attend",
    )(*[in_hbm(x) for x in (parents, queries, new_kv, gain, cache_kv)])


def beside(count):
    return 4 if count % 4 == 0 else min(count, 2)


def held_shape(gate, features, count):
    wide = beside(count)
    return pltpu.VMEM((count // wide, gate.shape[0], features * wide), BF16)


def column_copies(exchange, owners, gate, up, gate_held, up_held, sems):
    me = lax.axis_index("blk")
    features = gate.shape[1] // exchange.size
    wide = beside(len(owners))
    copies = []
    for n, (flip, p) in enumerate(owners):
        device = exchange.device(me, flip, p)
        columns = pl.ds(pl.multiple_of(device * features, features), features)
        place = pl.ds(n % wide * features, features)
        for k, (source, target) in enumerate(((gate, gate_held), (up, up_held))):
            copies.append(
                pltpu.make_async_copy(source.at[:, columns], target.at[n // wide, :, place], sems.at[2 * n + k])
            )
    return copies


def join_kernel(count, *refs):
    out = refs[-1]
    first = 0
    for part in refs[:count]:
        out[first : first + part.shape[0], :] = part[...]
        first += part.shape[0]


def join(parts, *after):
    rows = sum(p.shape[0] for p in parts)
    return pl.pallas_call(
        functools.partial(join_kernel, len(parts)),
        in_specs=[VMEM] * len(parts) + [ANY] * len(after),
        out_specs=VMEM,
        out_shape=pltpu.VMEM((rows,) + parts[0].shape[1:], parts[0].dtype),
        compiler_params=pltpu.CompilerParams(vmem_limit_bytes=2**20),
        name="join",
    )(*parts, *after)


def load_kernel(exchange, layout, unused, source, out, sems):
    copies = row_copies(exchange, layout, source, out, sems)
    for copy in copies:
        copy.start()
    for copy in copies:
        copy.wait()


def load_first_kernel(exchange, unused, weight, gate, up, weight_out, gate_out, up_out, sem, sems):
    copies = [pltpu.make_async_copy(weight, weight_out, sem)]
    copies += column_copies(exchange, [(0, 0)], gate, up, gate_out, up_out, sems)
    for copy in copies:
        copy.start()
    for copy in copies:
        copy.wait()


def row_copies(exchange, layout, source, out, sems):
    me = lax.axis_index("blk")
    flip, first, count = layout
    rows = source.shape[0] // exchange.size
    copies = []
    for k in range(count):
        device = exchange.device(me, flip, first + k)
        start = pl.multiple_of(device * rows, rows)
        place = pl.ds(k * rows, rows)
        copies.append(pltpu.make_async_copy(source.at[pl.ds(start, rows), :], out.at[place, :], sems.at[k]))
    return copies


def load(exchange, layout, after, source):
    rows = source.shape[0] // exchange.size * layout[2]
    return pl.pallas_call(
        functools.partial(load_kernel, exchange, layout),
        in_specs=[ANY, ANY],
        out_specs=VMEM,
        out_shape=pltpu.VMEM((rows, source.shape[1]), source.dtype),
        scratch_shapes=[pltpu.SemaphoreType.DMA((layout[2],))],
        compiler_params=pltpu.CompilerParams(vmem_limit_bytes=2**20),
        cost_estimate=pl.CostEstimate(flops=0, bytes_accessed=2 * rows * source.shape[1], transcendentals=0),
        name="load",
    )(after, in_hbm(source))


def load_columns_kernel(exchange, owners, unused, gate, up, gate_out, up_out, sems):
    copies = column_copies(exchange, owners, gate, up, gate_out, up_out, sems)
    for copy in copies:
        copy.start()
    for copy in copies:
        copy.wait()


def load_columns(exchange, owners, after, gate, up):
    held = held_shape(gate, gate.shape[1] // exchange.size, len(owners))
    return pl.pallas_call(
        functools.partial(load_columns_kernel, exchange, owners),
        in_specs=[ANY] * 3,
        out_specs=[VMEM] * 2,
        out_shape=[held, held],
        scratch_shapes=[pltpu.SemaphoreType.DMA((2 * len(owners),))],
        compiler_params=pltpu.CompilerParams(vmem_limit_bytes=2**20),
        cost_estimate=pl.CostEstimate(flops=0, bytes_accessed=5 * 2**20, transcendentals=0),
        name="load_columns",
    )(after, in_hbm(gate), in_hbm(up))


def load_first(exchange, after, weight, gate, up):
    own = held_shape(gate, gate.shape[1] // exchange.size, 1)
    return pl.pallas_call(
        functools.partial(load_first_kernel, exchange),
        in_specs=[ANY] * 4,
        out_specs=[VMEM] * 3,
        out_shape=[pltpu.VMEM(weight.shape, weight.dtype), own, own],
        scratch_shapes=[pltpu.SemaphoreType.DMA, pltpu.SemaphoreType.DMA((2,))],
        compiler_params=pltpu.CompilerParams(vmem_limit_bytes=2**20),
        cost_estimate=pl.CostEstimate(
            flops=0, bytes_accessed=2 * weight.shape[0] * weight.shape[1], transcendentals=0
        ),
        name="load_first",
    )(after, in_hbm(weight), in_hbm(gate), in_hbm(up))


def project_kernel(exchange, layout, owners, rows, steps, *refs):
    pieces = refs[: len(layout)]
    residual, weight, gate, up, down, out, copy_out, gains, gate_out, up_out, rows_out = refs[len(layout) :][:11]
    wide, packed, stream, stream_sem, ahead_sems, row_sems = refs[len(layout) :][11:]
    per_device = wide.shape[0] // exchange.size
    block = per_device + GAIN_ROWS
    beam_rows = out.shape[0]
    step = weight.shape[1] // steps
    stream_copy = pltpu.make_async_copy(residual, stream, stream_sem)
    stream_copy.start()
    fetches = column_copies(exchange, owners, gate, up, gate_out, up_out, ahead_sems)
    fetches += row_copies(exchange, rows, down, rows_out, row_sems)
    for copy in fetches:
        copy.start()

    @apart
    def _():
        me = lax.axis_index("blk")
        for piece, (flip, first, count) in zip(pieces, layout):
            for k in range(count):
                device = exchange.device(me, flip, first + k)
                start = pl.multiple_of(device * per_device, per_device)
                wide[pl.ds(start, per_device), :] = piece[k * block : k * block + per_device, :].astype(F32)
                scaling = piece[k * block + per_device : (k + 1) * block, :].astype(F32)
                slot = flip * exchange.half + first + k
                gains[slot : slot + 1, :] = jnp.concatenate(
                    [scaling[j : j + 1, :] for j in range(gains.shape[1] // HD)], axis=1
                )
        for h in range(HQ):
            packed[:, h * HD : (h + 1) * HD] = wide[pl.ds(h, beam_rows, stride=HQ), :].astype(BF16)
        summed = None
        for s in range(steps):
            part = slice(s * step, (s + 1) * step)
            term = lax.dot_general(packed[:, part], weight[:, part], NT, preferred_element_type=F32)
            summed = term if summed is None else summed + term
        stream_copy.wait()
        result = (stream[...].astype(F32) + summed).astype(BF16)
        out[...] = result
        copy_out[...] = result
        for copy in fetches:
            copy.wait()


def project(exchange, pieces, residual, weight, gate, up, owners, down, rows):
    beam_rows, features = residual.shape
    layout = [p[1:] for p in pieces]
    return pl.pallas_call(
        functools.partial(project_kernel, exchange, layout, owners, rows, 4),
        in_specs=[VMEM] * len(pieces) + [ANY, VMEM, ANY, ANY, ANY],
        out_specs=[VMEM] * 6,
        out_shape=[
            jax.ShapeDtypeStruct((beam_rows, features), BF16),
            pltpu.VMEM((beam_rows, features), BF16),
            pltpu.VMEM((exchange.size, features), F32),
            held_shape(gate, features, len(owners)),
            held_shape(gate, features, len(owners)),
            pltpu.VMEM((rows[2] * features, gate.shape[0]), BF16),
        ],
        scratch_shapes=[
            pltpu.VMEM((beam_rows * HQ, HD), F32),
            pltpu.VMEM((beam_rows, HQ * HD), BF16),
            pltpu.VMEM((beam_rows, features), BF16),
            pltpu.SemaphoreType.DMA,
            pltpu.SemaphoreType.DMA((2 * len(owners),)),
            pltpu.SemaphoreType.DMA((rows[2],)),
        ],
        compiler_params=pltpu.CompilerParams(vmem_limit_bytes=8 * 2**20),
        cost_estimate=pl.CostEstimate(flops=4 * 10**8, bytes_accessed=9 * 2**20, transcendentals=0),
        name="project",
    )(*[p[0] for p in pieces], in_hbm(residual), weight, in_hbm(gate), in_hbm(up), in_hbm(down))


def enter_kernel(exchange, layout, begun, groups, ahead, rows, *refs):
    refs = list(refs)
    take = lambda n: [refs.pop(0) for _ in range(n)]
    blocks = take(len(layout))
    (gains,) = take(1)
    sums = take(3) if begun else None
    held = [take(2) for _ in groups]
    gate, up = take(2)
    down = take(1)[0] if rows else None
    gate_sum, up_sum, squares = take(3)
    beam_rows, features = blocks[0].shape[0] // layout[0][2], blocks[0].shape[1]
    owners = [
        (block, k, flip, first + k) for block, (flip, first, count) in zip(blocks, layout) for k in range(count)
    ]
    chunks = []
    for pair, count in zip(held, groups):
        wide = beside(count)
        for n in range(count // wide):
            chunks.append((pair, n, [owners.pop(0) for _ in range(wide)]))
    ahead_out = take(2) if ahead else None
    rows_out = take(1)[0] if rows else None
    copies = column_copies(exchange, ahead, gate, up, *ahead_out, refs.pop(0)) if ahead else []
    if rows:
        copies += row_copies(exchange, rows, down, rows_out, refs.pop(0))
    for copy in copies:
        copy.start()

    @apart
    def _():
        total = sums[2][...] if begun else jnp.zeros((beam_rows, features), F32)
        for c, (pair, slot, members) in enumerate(chunks):
            parts = []
            for block, k, flip, p in members:
                value = block[k * beam_rows : (k + 1) * beam_rows, :].astype(F32)
                total += value * value
                row = flip * exchange.half + p
                parts.append((value * gains[row : row + 1, :]).astype(BF16))
            normed = jnp.concatenate(parts, axis=1) if len(parts) > 1 else parts[0]
            depth = len(parts) * features
            for which, result in ((0, gate_sum), (1, up_sum)):
                term = lax.dot_general(normed, pair[which][slot, :, :depth], NT, preferred_element_type=F32)
                if c:
                    result[...] += term
                elif begun:
                    result[...] = sums[which][...] + term
                else:
                    result[...] = term
        squares[...] = total
        for copy in copies:
            copy.wait()


def enter(exchange, blocks, gains, sums, held, gate, up, ahead=(), down=None, rows=None):
    layout = [b[1:] for b in blocks]
    beam_rows, features = blocks[0][0].shape[0] // blocks[0][3], blocks[0][0].shape[1]
    units = gate.shape[0]
    count = sum(b[3] for b in blocks)
    out_shape = [
        pltpu.VMEM((beam_rows, units), F32),
        pltpu.VMEM((beam_rows, units), F32),
        pltpu.VMEM((beam_rows, features), F32),
    ]
    scratch = []
    if ahead:
        out_shape += [held_shape(gate, features, len(ahead))] * 2
        scratch.append(pltpu.SemaphoreType.DMA((2 * len(ahead),)))
    operands = [b[0] for b in blocks] + [gains] + list(sums or ()) + [x for h in held for x in h[:2]]
    in_specs = [VMEM] * len(operands) + [ANY] * 2
    operands += [in_hbm(gate), in_hbm(up)]
    if rows:
        operands.append(in_hbm(down))
        in_specs.append(ANY)
        out_shape.append(pltpu.VMEM((down.shape[0] // exchange.size * rows[2], units), BF16))
        scratch.append(pltpu.SemaphoreType.DMA((rows[2],)))
    return pl.pallas_call(
        functools.partial(enter_kernel, exchange, layout, sums is not None, [h[2] for h in held], ahead, rows),
        in_specs=in_specs,
        out_specs=[VMEM] * len(out_shape),
        out_shape=out_shape,
        scratch_shapes=scratch,
        compiler_params=pltpu.CompilerParams(vmem_limit_bytes=4 * 2**20),
        cost_estimate=pl.CostEstimate(
            flops=count * 4 * beam_rows * units * features,
            bytes_accessed=count * 4 * units * features,
            transcendentals=0,
        ),
        name="enter",
    )(*operands)


def leave_kernel(exchange, first, rows, *refs):
    refs = list(refs)
    take = lambda n: [refs.pop(0) for _ in range(n)]
    inputs = take(3 if first else 1)
    held, down, _ = take(3)
    (out,) = take(1)
    hidden = take(1)[0] if first else inputs[0]
    copies = row_copies(exchange, rows, down, *refs) if rows else []
    for copy in copies:
        copy.start()

    @apart
    def _():
        if first:
            gate_sum, up_sum, squares = inputs
            mean = jnp.sum(squares[...], axis=1, keepdims=True) / D
            inverse_rms = lax.rsqrt(mean + epsilon)
            hidden[...] = (jax.nn.silu(gate_sum[...] * inverse_rms) * (up_sum[...] * inverse_rms)).astype(BF16)
        count, _, features = out.shape
        wide = beside(count)
        for n in range(0, count, wide):
            term = lax.dot_general(
                hidden[...], held[n * features : (n + wide) * features, :], NT, preferred_element_type=F32
            )
            for j in range(wide):
                out[n + j] = term[:, j * features : (j + 1) * features].astype(out.dtype)
        for copy in copies:
            copy.wait()


def leave(exchange, inputs, held, features, dtype, down, rows, after):
    first = len(inputs) == 3
    beam_rows, units = inputs[0].shape
    count = held.shape[0] // features
    out_shape = [pltpu.VMEM((count, beam_rows, features), dtype)]
    if first:
        out_shape.append(pltpu.VMEM((beam_rows, units), BF16))
    scratch = []
    if rows:
        out_shape.append(pltpu.VMEM((rows[2] * features, units), BF16))
        scratch.append(pltpu.SemaphoreType.DMA((rows[2],)))
    return pl.pallas_call(
        functools.partial(leave_kernel, exchange, first, rows),
        in_specs=[VMEM] * (len(inputs) + 1) + [ANY] * 2,
        out_specs=[VMEM] * len(out_shape),
        out_shape=out_shape,
        scratch_shapes=scratch,
        compiler_params=pltpu.CompilerParams(vmem_limit_bytes=4 * 2**20),
        cost_estimate=pl.CostEstimate(flops=0, bytes_accessed=2**10, transcendentals=0),
        name="leave",
    )(*inputs, held, in_hbm(down), after)


def leave_pair_kernel(exchange, rows, hidden, send_rows, keep_rows, down, unused, send, keep, *refs):
    copies = row_copies(exchange, rows, down, *refs) if rows else []
    for copy in copies:
        copy.start()
    count, _, features = send.shape

    @apart
    def _():
        for held, out in ((send_rows, send), (keep_rows, keep)):
            term = lax.dot_general(hidden[...], held[...], NT, preferred_element_type=F32)
            for j in range(count):
                out[j] = term[:, j * features : (j + 1) * features].astype(out.dtype)
        for copy in copies:
            copy.wait()


def leave_pair(exchange, hidden, send_rows, keep_rows, down, rows, after):
    beam_rows, units = hidden.shape
    features = down.shape[0] // exchange.size
    count = send_rows.shape[0] // features
    out_shape = [
        pltpu.VMEM((count, beam_rows, features), BF16),
        pltpu.VMEM((count, beam_rows, features), F32),
    ]
    scratch = []
    if rows:
        out_shape.append(pltpu.VMEM((rows[2] * features, units), BF16))
        scratch.append(pltpu.SemaphoreType.DMA((rows[2],)))
    return pl.pallas_call(
        functools.partial(leave_pair_kernel, exchange, rows),
        in_specs=[VMEM] * 3 + [ANY] * 2,
        out_specs=[VMEM] * len(out_shape),
        out_shape=out_shape,
        scratch_shapes=scratch,
        compiler_params=pltpu.CompilerParams(vmem_limit_bytes=4 * 2**20),
        cost_estimate=pl.CostEstimate(flops=0, bytes_accessed=2**10, transcendentals=0),
        name="leave_pair",
    )(hidden, send_rows, keep_rows, in_hbm(down), after)


def fold_kernel(kept, *refs):
    total = kept[...]
    for passed in refs[:-1]:
        total += passed[...].astype(F32)
    refs[-1][...] = total


def fold(kept, *passed):
    return pl.pallas_call(
        fold_kernel,
        in_specs=[VMEM] * (1 + len(passed)),
        out_specs=VMEM,
        out_shape=pltpu.VMEM(kept.shape, F32),
        compiler_params=pltpu.CompilerParams(vmem_limit_bytes=2**20),
        name="fold",
    )(kept, *passed)


def fast_shards(size, queries, new_kv, cache_kv, parents, residual, out_proj, norm_gain, w_gate, w_up, w_down):
    exchange = Exchange(size)
    features = residual.shape[0]
    high = (4, 4)

    mixed = attend(parents, queries, new_kv, cache_kv, norm_gain)
    fresh = exchange.swap(mixed, 0)
    high_send = load(exchange, (1,) + high, mixed, w_down)
    have = join([mixed, fresh], high_send)
    fresh = exchange.swap(have, 1)
    held3 = load_columns(exchange, [(1, 0), (1, 1)], have, w_gate, w_up)
    have = join([have, fresh], held3[0])
    other = exchange.swap_core(have)
    fresh = exchange.swap(have, 2)
    weight, *held0 = load_first(exchange, have, out_proj, w_gate, w_up)
    fresh = join([fresh], weight, other)
    pieces = [(have, 0, 0, 4), (other, 1, 0, 4), (fresh, 0, 4, 4), (exchange.swap_core(fresh), 1, 4, 4)]
    after, have, gains, *held1, send_rows2 = project(
        exchange, pieces, residual.T, weight, w_gate, w_up, [(0, 1)], w_down, (1, 2, 2)
    )

    block0 = have
    fresh1 = exchange.swap(block0, 0)
    *sums, g, u = enter(
        exchange, [(block0, 0, 0, 1)], gains, None, [(*held0, 1)], w_gate, w_up, [(0, 2), (0, 3)]
    )
    held2 = (g, u, 2)
    have = join([block0, fresh1], sums[2])
    other1 = exchange.swap_core(have)
    fresh2 = exchange.swap(have, 1)
    *sums, g, u = enter(
        exchange, [(fresh1, 0, 1, 1)], gains, sums, [(*held1, 1)], w_gate, w_up, [(1, 2), (1, 3)]
    )
    held4 = (g, u, 2)
    have = join([have, fresh2], sums[2], other1)
    other2 = exchange.swap_core(fresh2)
    fresh3 = exchange.swap(have, 2)
    *sums, g, u = enter(
        exchange,
        [(fresh2, 0, 2, 2), (other1, 1, 0, 2)],
        gains, sums, [held2, (*held3, 2)], w_gate, w_up, [(0, 4), (0, 5), (0, 6), (0, 7)],
    )
    held5 = (g, u, 4)
    fresh3 = join([fresh3], sums[2], other2)
    other3 = exchange.swap_core(fresh3)
    *sums, g, u = enter(
        exchange,
        [(other2, 1, 2, 2), (fresh3, 0, 4, 4)],
        gains, sums, [held4, held5], w_gate, w_up, [(1, 4), (1, 5), (1, 6), (1, 7)],
    )
    *sums, high_keep = enter(
        exchange, [(other3, 1, 4, 4)], gains, sums, [(g, u, 4)], w_gate, w_up, (), w_down, (0,) + high
    )

    send, hidden, keep_rows2 = leave(exchange, sums, high_send, features, BF16, w_down, (0, 2, 2), sums[2])
    received = exchange.swap_core(send).astype(F32)
    keep, keep_rows0 = leave(exchange, (hidden,), high_keep, features, F32, w_down, (0, 0, 2), send)
    onward = (keep + received).astype(BF16)
    passed2 = exchange.swap(onward[2:], 2)
    passed0 = exchange.swap(onward[:2], 2)
    send, keep, send_rows0 = leave_pair(exchange, hidden, send_rows2, keep_rows2, w_down, (1, 0, 2), onward)
    received = exchange.swap_core(send).astype(F32)
    onward = (fold(keep, passed2) + received).astype(BF16)
    passed1 = exchange.swap(onward, 1)
    send, keep = leave_pair(exchange, hidden, send_rows0, keep_rows0, w_down, None, onward)
    received = exchange.swap_core(send).astype(F32)
    keep = fold(keep, passed0, passed1) + received
    keep = keep[0] + exchange.swap(keep[1].astype(BF16), 0).astype(F32)
    layer_out = (after.astype(F32) + keep).astype(BF16)
    return (after.T, layer_out.T)


def solution(mesh):
    size = mesh.shape["blk"]

    def shards(*args):
        features, beam_rows = args[4].shape
        units = args[7].shape[0]
        fits = (
            size == 16
            and features % HD == 0
            and features // HD <= GAIN_ROWS
            and beam_rows % 16 == 0
            and beam_rows * HQ * HD <= 2**20
            and units % HD == 0
            and units * features <= 2**20
        )
        return functools.partial(fast_shards, size)(*args) if fits else plain_shards(*args)

    return jax.shard_map(
        shards,
        mesh=mesh,
        in_specs=(
            P(("groups", "blk"), None),
            P(("groups", "blk"), None, None),
            P(("groups", "blk"), None, None, None),
            P(("groups", "blk")),
            P("blk", "groups"),
            P("blk", None),
            P("blk"),
            P("blk", None),
            P("blk", None),
            P(None, "blk"),
        ),
        out_specs=(P("blk", "groups"), P("blk", "groups")),
        check_vma=False,
    )
```
